256 devices in a mesh: dp: 4 (over x_lo, core), ctx: 64 (over y, x_hi, z).
Axes of the slice: x: 4 (x_hi: 2, x_lo: 2; x = x_hi * 2 + x_lo), y: 4, z: 8, core: 2. Of those that a mesh axis runs over, the one named last changes fastest.
Arguments:
- queries: bfloat16 [4, 2048, 2048], P('dp', 'ctx'), may hold values from -8 to 8
- keys: bfloat16 [4, 2048, 512], P('dp', 'ctx'), may hold values from -8 to 8
- values: bfloat16 [4, 2048, 512], P('dp', 'ctx'), may hold values from -6 to 6
- out_grad: bfloat16 [4, 2048, 2048], P('dp', 'ctx'), may hold values from -6 to 6
- routed_inputs: bfloat16 [4, 2048, 4096], P('dp', 'ctx'), may hold values from -6 to 6
- router_weight: float32 [4096], replicated, may hold values from -0.09375 to 0.09375
- positions: int32 [4, 2048], P('dp', 'ctx'), may hold values from 0 to 16383, as said below
Outputs:
- query_grad: bfloat16 [4, 2048, 2048], P('dp', 'ctx')
- key_grad: bfloat16 [4, 2048, 512], P('dp', 'ctx')
- value_grad: bfloat16 [4, 2048, 512], P('dp', 'ctx')
- router_grad: float32 [4096], replicated
The draws below stay inside these ranges and needn't reach their ends.
Inputs may be any that keep to these rules, and one draw needn't show every extreme that they name: `positions`: within each sequence strictly increasing, the first 0 and the last 16383.
All inputs are finite; a program needn't handle non-finite values.
Results may differ from the reference program's by a relative error of at most 0.039.
Values may be sent and summed in bfloat16 or wider, within the bound.
A program may use at most 128 MiB of HBM per device.

```python
import math
import jax
import jax.numpy as jnp
from jax import lax

D = 4096
HQ = 16
KVH = 4
HD = 128
SEQS = 4
SEL = 2048
CTX = 16384


def draw_queries(key, part):
    key = jax.random.fold_in(key, 1)
    full_shape = (SEQS, SEL, HQ * HD)
    result = jnp.clip(jax.random.normal(key, full_shape, jnp.float32), -6.0, 6.0)
    return result.astype(jnp.bfloat16)


def draw_keys(key, part):
    key = jax.random.fold_in(key, 2)
    full_shape = (SEQS, SEL, KVH * HD)
    result = jnp.clip(jax.random.normal(key, full_shape, jnp.float32), -6.0, 6.0)
    return result.astype(jnp.bfloat16)


def draw_positions(key, part):
    key = jax.random.fold_in(key, 3)
    sequences = []
    for sequence in range(SEQS):
        picked = jax.random.permutation(jax.random.fold_in(key, sequence), CTX - 2)[:SEL - 2] + 1
        complete = jnp.concatenate([jnp.zeros((1,), jnp.int32), picked.astype(jnp.int32), jnp.full((1,), CTX - 1, jnp.int32)])
        sequences.append(jnp.sort(complete))
    return jnp.stack(sequences)


def shard_levels(own_key, shape, cuts, low, top_value):
    gain = 1.0
    for axis_at, parts in cuts:
        steps = jax.random.uniform(jax.random.fold_in(jax.random.fold_in(own_key, 6), axis_at), (parts,), jnp.float32, low / len(cuts), top_value / len(cuts))
        gain = gain * jnp.repeat(jnp.exp(steps), shape[axis_at] // parts).reshape((-1,) + (1,) * (len(shape) - 1 - axis_at))
    return gain


def bell_draw(key, extent, width, reach, cuts=(), held_as=jnp.bfloat16):
    values = width * jax.random.normal(key, extent, jnp.float32)
    if cuts:
        values = values * shard_levels(key, extent, cuts, -0.22, 0.18)
    return jnp.clip(values, -reach, reach).astype(held_as)


def setup_inputs(seed: int = 0) -> dict:
    streams_of = jax.random.split(jax.random.key(seed), 8)
    queries = draw_queries(jax.random.fold_in(streams_of[7], 71), 0)
    keys = draw_keys(jax.random.fold_in(streams_of[7], 71), 0)
    values = bell_draw(streams_of[2], (SEQS, SEL, KVH * HD), 1.0, 6.0, ((0, 4), (1, 64)))
    out_grad = bell_draw(streams_of[3], (SEQS, SEL, HQ * HD), 1.0, 6.0, ((0, 4), (1, 64)))
    routed_inputs = bell_draw(streams_of[4], (SEQS, SEL, D), 1.0, 6.0, ((0, 4), (1, 64)))
    router_weight = bell_draw(streams_of[5], (D,), D ** -0.5, 0.09375, (), jnp.float32)
    positions = draw_positions(jax.random.fold_in(streams_of[7], 71), 0)
    return {"queries": queries, "keys": keys, "values": values, "out_grad": out_grad, "routed_inputs": routed_inputs, "router_weight": router_weight, "positions": positions}


ROPE_BASE = 500000.0

def rope_tables(pair_count):
    frequency = [ROPE_BASE ** (-number / pair_count) for number in range(pair_count)]
    coarse = [256.0 * factor % (2.0 * math.pi) for factor in frequency]
    return (jnp.asarray(frequency, jnp.float32), jnp.asarray(coarse, jnp.float32))

def rotation(positions, head_dim):
    frequency, coarse = rope_tables(head_dim // 2)
    upper_part = (positions // 256).astype(jnp.float32)
    lower_part = (positions % 256).astype(jnp.float32)
    angles = upper_part[:, None] * coarse[None, :] + lower_part[:, None] * frequency[None, :]
    return (jnp.cos(angles)[:, None, :], jnp.sin(angles)[:, None, :])

def turn_forward(vectors, cosine, sine):
    width_half = vectors.shape[-1] // 2
    first_half = vectors[..., :width_half]
    second_half = vectors[..., width_half:]
    return jnp.concatenate([first_half * cosine - second_half * sine, second_half * cosine + first_half * sine], axis=-1)

def turn_back(vectors, cosine, sine):
    width_half = vectors.shape[-1] // 2
    first_half = vectors[..., :width_half]
    second_half = vectors[..., width_half:]
    return jnp.concatenate([first_half * cosine + second_half * sine, second_half * cosine - first_half * sine], axis=-1)

def one_sequence(queries, keys, values, out_grad, inputs, router_weight, positions):
    group_size = HQ // KVH
    score_scale = 1.0 / math.sqrt(HD)
    cosine, sine = rotation(positions, HD)
    query_rot = turn_forward(queries.astype(jnp.float32).reshape(SEL, HQ, HD), cosine, sine).astype(jnp.bfloat16)
    key_rot = turn_forward(keys.astype(jnp.float32).reshape(SEL, KVH, HD), cosine, sine).astype(jnp.bfloat16)
    key_wide = key_rot.astype(jnp.float32)
    value_wide = values.reshape(SEL, KVH, HD).astype(jnp.float32)
    logits = jnp.dot(inputs.astype(jnp.float32), router_weight, precision=lax.Precision.HIGHEST)
    gate = jax.nn.sigmoid(logits)
    upstream = out_grad.astype(jnp.float32).reshape(SEL, KVH, group_size, HD)
    scaled_grad = (gate[:, None, None, None] * upstream).astype(jnp.bfloat16)
    rows_block = min(512, SEL)
    blocks = SEL // rows_block

    def split(array):
        return array.reshape((blocks, rows_block) + array.shape[1:])

    def step(carry, pieces):
        key_acc, value_acc = carry
        query_tile, scaled_tile, upstream_tile, place_tile, gate_tile = pieces
        query_wide = query_tile.astype(jnp.float32)
        scaled_wide = scaled_tile.astype(jnp.float32)
        scores = jnp.einsum('tkgd,ukd->kgtu', query_wide, key_wide) * score_scale
        allowed = place_tile[:, None] >= positions[None, :]
        scores = jnp.where(allowed[None, None], scores, -jnp.inf)
        top = lax.optimization_barrier(jnp.max(scores, axis=-1, keepdims=True))
        lse = top + jnp.log(lax.optimization_barrier(jnp.sum(jnp.exp(scores - top), axis=-1, keepdims=True)))
        weights = jnp.exp(scores - lse)
        probs = lax.optimization_barrier(weights.astype(jnp.bfloat16)).astype(jnp.float32)
        attn = jnp.einsum('kgtu,ukd->tkgd', probs, value_wide)
        router_term = lax.optimization_barrier(jnp.sum(upstream_tile * attn, axis=(1, 2, 3)))
        logit_grad = gate_tile * (1.0 - gate_tile) * router_term
        delta = jnp.transpose(lax.optimization_barrier(jnp.sum(scaled_wide * attn, axis=-1)), (1, 2, 0))
        prob_grad = jnp.einsum('tkgd,ukd->kgtu', scaled_wide, value_wide)
        score_grad = (weights * (prob_grad - delta[..., None]) * score_scale).astype(jnp.bfloat16)
        score_wide = lax.optimization_barrier(score_grad).astype(jnp.float32)
        query_acc = jnp.einsum('kgtu,ukd->tkgd', score_wide, key_wide)
        key_acc = key_acc + jnp.einsum('kgtu,tkgd->ukd', score_wide, query_wide)
        value_acc = value_acc + jnp.einsum('kgtu,tkgd->ukd', probs, scaled_wide)
        return ((key_acc, value_acc), (query_acc, logit_grad))
    start_state = (jnp.zeros((SEL, KVH, HD), jnp.float32), jnp.zeros((SEL, KVH, HD), jnp.float32))
    pieces = (split(query_rot.reshape(SEL, KVH, group_size, HD)), split(scaled_grad), split(upstream), split(positions), split(gate))
    (key_acc, value_acc), (query_acc, logit_grad) = lax.scan(step, start_state, pieces)
    query_acc = query_acc.reshape(SEL, HQ, HD)
    logit_grad = logit_grad.reshape(SEL)
    query_grad = turn_back(query_acc, cosine, sine).astype(jnp.bfloat16).reshape(SEL, HQ * HD)
    key_grad = turn_back(key_acc, cosine, sine).astype(jnp.bfloat16).reshape(SEL, KVH * HD)
    value_grad = value_acc.astype(jnp.bfloat16).reshape(SEL, KVH * HD)
    router_part = jnp.dot(logit_grad, inputs.astype(jnp.float32), precision=lax.Precision.HIGHEST)
    return (query_grad, key_grad, value_grad, router_part)

def reference(queries, keys, values, out_grad, routed_inputs, router_weight, positions):
    query_list = []
    key_list = []
    value_list = []
    router_total = jnp.zeros((D,), jnp.float32)
    for sequence in range(SEQS):
        query_grad, key_grad, value_grad, router_part = one_sequence(queries[sequence], keys[sequence], values[sequence], out_grad[sequence], routed_inputs[sequence], router_weight, positions[sequence])
        query_list.append(query_grad)
        key_list.append(key_grad)
        value_list.append(value_grad)
        router_total = router_total + router_part
    router_grad = router_total / math.sqrt(SEQS * SEL)
    return (jnp.stack(query_list), jnp.stack(key_list), jnp.stack(value_list), router_grad)
```

```python
import math

import jax
import jax.numpy as jnp
import numpy as np
from jax import lax
from jax.experimental import pallas as pl
from jax.experimental.pallas import tpu as pltpu
from jax.sharding import PartitionSpec as P

HQ = 16
KVH = 4
HD = 128
ROPE_BASE = 500000.0
SCORE_SCALE = 1.0 / math.sqrt(HD)
MESH = pl.DeviceIdType.MESH

ROWS = 32
QUAD = 4
MATES = 16
SUPER = 8
SLOT = QUAD * ROWS
SPAN = 2 * SLOT
GROUP = HQ // KVH
QROWS = GROUP * SLOT
NEG = -1e30
F32 = jnp.float32
BF16 = jnp.bfloat16


def rope_rows():
    pairs = HD // 2
    frequency = [ROPE_BASE ** (-number / pairs) for number in range(pairs)]
    coarse = [256.0 * factor % (2.0 * math.pi) for factor in frequency]
    table = np.zeros((8, HD), np.float32)
    table[0] = np.asarray(frequency + frequency, np.float32)
    table[1] = np.asarray(coarse + coarse, np.float32)
    return table


def nt(left, right):
    return lax.dot_general(left, right, (((1,), (1,)), ((), ())), preferred_element_type=F32)


def tn(left, right):
    return lax.dot_general(left, right, (((0,), (0,)), ((), ())), preferred_element_type=F32)


def kernel(
    q_ref, k_ref, v_ref, g_ref, x_ref, w_ref, p_ref, rope_ref,
    dq_out, dk_out, dv_out, r_out,
    cos_s, sin_s, gate_s, kv4, qg4, kv, qg, q_s, g_s, s_s, d_s, dqt_s, pb, rb, dqs, dqr, cb, kr,
    ts, tr, rp, r1, r2s, r2, r3s, r3, r4,
    kv_ss, kv_rs, qg_ss, qg_rs, ga_ss, ga_rs, pb_ss, pb_rs, dq_ss, dq_rs, kr_ss, kr_rs,
    t_ss, t_rs, r1_ss, r1_rs, r2_ss, r2_rs, r3_ss, r3_rs, r4_ss, r4_rs,
):
    dp = lax.axis_index("dp")
    ctx = lax.axis_index("ctx")
    run = ctx // 8
    z = ctx % 8
    head = z // 2
    par = z % 2
    mate = run * 2 + par

    def quad_at(member):
        return (dp, run * 8 + 2 * member + par)

    def mate_at(index):
        return (dp, (index // 2) * 8 + 2 * head + index % 2)

    def dp_at(index):
        return (index, ctx)

    def remote(src, dst, send, recv, to):
        return pltpu.make_async_remote_copy(
            src_ref=src, dst_ref=dst, send_sem=send, recv_sem=recv, device_id=to, device_id_type=MESH
        )

    def other(step):
        return lax.rem(head + step, QUAD)

    def other_dp(step):
        return lax.rem(dp + step, 4)

    barrier = pltpu.get_barrier_semaphore()
    for step in range(1, QUAD):
        pl.semaphore_signal(barrier, inc=1, device_id=quad_at(other(step)), device_id_type=MESH)
        pl.semaphore_signal(barrier, inc=1, device_id=dp_at(other_dp(step)), device_id_type=MESH)

    def greet(step, carry):
        pl.semaphore_signal(
            barrier, inc=1, device_id=mate_at(lax.rem(mate + step, MATES)), device_id_type=MESH
        )
        return carry

    lax.fori_loop(1, MATES, greet, 0)

    eye = lax.broadcasted_iota(jnp.int32, (ROWS, ROWS), 0) == lax.broadcasted_iota(
        jnp.int32, (ROWS, ROWS), 1
    )
    places = jnp.broadcast_to(p_ref[...], (ROWS, ROWS))
    upper = jnp.sum(jnp.where(eye, (places >> 8).astype(F32), 0.0), axis=1, keepdims=True)
    lower = jnp.sum(jnp.where(eye, (places & 255).astype(F32), 0.0), axis=1, keepdims=True)
    angles = upper * rope_ref[1:2, :] + lower * rope_ref[0:1, :]
    lane = lax.broadcasted_iota(jnp.int32, (ROWS, HD), 1)
    cos = jnp.cos(angles)
    sin = jnp.sin(angles)
    sin = jnp.where(lane < HD // 2, -sin, sin)
    cos_s[...] = cos
    sin_s[...] = sin

    def turn(rows):
        return rows * cos + pltpu.roll(rows, HD // 2, 1) * sin

    for number in range(KVH):
        cols = slice(number * HD, (number + 1) * HD)
        kv4[number, :, :HD] = turn(k_ref[:, cols].astype(F32)).astype(BF16)
        kv4[number, :, HD:] = v_ref[:, cols]

    pl.semaphore_wait(barrier, 2 * (QUAD - 1) + MATES - 1)

    def kv_copy(step):
        to = other(step)
        return remote(
            kv4.at[to], kv.at[mate, pl.ds(head * ROWS, ROWS)], kv_ss.at[step], kv_rs.at[step], quad_at(to)
        )

    for step in range(1, QUAD):
        kv_copy(step).start()
    kv[mate, pl.ds(pl.multiple_of(head * ROWS, ROWS), ROWS)] = kv4[head]

    logits = jnp.sum(x_ref[...].astype(F32) * w_ref[...], axis=1, keepdims=True)
    gate = jax.nn.sigmoid(logits)
    gate_s[...] = jnp.broadcast_to(gate, (ROWS, HD))
    for number in range(HQ):
        cols = slice(number * HD, (number + 1) * HD)
        part, into = number // GROUP, slice((number % GROUP) * HD, (number % GROUP + 1) * HD)
        qg4[part, 0, :, into] = turn(q_ref[:, cols].astype(F32)).astype(BF16)
        qg4[part, 1, :, into] = (gate * g_ref[:, cols].astype(F32)).astype(BF16)

    def qg_copy(step):
        to = other(step)
        return remote(qg4.at[to], qg.at[head], qg_ss.at[step], qg_rs.at[step], quad_at(to))

    for step in range(1, QUAD):
        qg_copy(step).start()
    qg[head] = qg4[head]

    for step in range(1, QUAD):
        kv_copy(step).wait_recv()

    def ga_send(index):
        return remote(kv.at[mate], kv.at[mate], ga_ss.at[index], ga_rs.at[mate], mate_at(index))

    def ga_recv(index):
        return remote(kv.at[mate], kv.at[index], ga_ss.at[index], ga_rs.at[index], mate_at(index))

    def ga_start(index, carry):
        @pl.when(index != mate)
        def _():
            ga_send(index).start()

        return carry

    lax.fori_loop(run * 2, MATES, ga_start, 0)

    for step in range(1, QUAD):
        qg_copy(step).wait_recv()
    for number in range(GROUP):
        cols = slice(number * HD, (number + 1) * HD)
        q_s[number * SLOT : (number + 1) * SLOT, :] = qg[:, 0, :, cols].reshape(SLOT, HD)
        g_s[number * SLOT : (number + 1) * SLOT, :] = qg[:, 1, :, cols].reshape(SLOT, HD)

    key_at = lax.broadcasted_iota(jnp.int32, (SPAN, QROWS), 0)
    key_at = (key_at >> 7) * ROWS + ((key_at & 96) << 1) + (key_at & 31)
    row_at = lax.broadcasted_iota(jnp.int32, (SPAN, QROWS), 1)
    row_at = par * ROWS + ((row_at & 96) << 1) + (row_at & 31)
    ahead = key_at - row_at

    def score_step(number, top):
        for side in range(2):
            index = 2 * number + side

            @pl.when(index != mate)
            def _():
                ga_recv(index).wait_recv()

        both = jnp.concatenate([kv[2 * number], kv[2 * number + 1]], axis=0)
        scores = nt(both[:, :HD], q_s[...]) * (SCORE_SCALE * math.log2(math.e))
        scores = jnp.where(ahead <= (run - number) * SPAN, scores, NEG)
        s_s[number] = scores
        d_s[number] = nt(both[:, HD:], g_s[...]) * SCORE_SCALE
        return jnp.maximum(top, jnp.max(scores, axis=0, keepdims=True))

    top = lax.fori_loop(0, run + 1, score_step, jnp.full((1, QROWS), NEG, F32))

    def mass_step(number, carry):
        mass, pull = carry
        raised = jnp.exp2(s_s[number] - top)
        s_s[number] = raised
        return (
            mass + jnp.sum(raised, axis=0, keepdims=True),
            pull + jnp.sum(raised * d_s[number], axis=0, keepdims=True),
        )

    zero_row = jnp.zeros((1, QROWS), F32)
    mass, pull = lax.fori_loop(0, run + 1, mass_step, (zero_row, zero_row))
    inverse = 1.0 / mass
    delta = pull * inverse

    term = delta[:, :SLOT]
    for number in range(1, GROUP):
        term = term + delta[:, number * SLOT : (number + 1) * SLOT]
    ts[...] = jnp.broadcast_to(term * math.sqrt(HD), (8, SLOT))

    def t_copy(step):
        return remote(ts, tr.at[head], t_ss.at[step], t_rs.at[step], quad_at(other(step)))

    for step in range(1, QUAD):
        t_copy(step).start()
    tr[head] = ts[...]

    def pb_send(index):
        return remote(pb.at[index], rb.at[mate], pb_ss.at[index], pb_rs.at[mate], mate_at(index))

    def pb_recv(index):
        return remote(pb.at[index], rb.at[index], pb_ss.at[index], pb_rs.at[index], mate_at(index))

    dqt_s[...] = jnp.zeros_like(dqt_s)

    def grad_step(number, carry):
        weights = s_s[number] * inverse
        probs = weights.astype(BF16)
        slope = (weights * (d_s[number] - delta)).astype(BF16)
        keys = jnp.concatenate([kv[2 * number, :, :HD], kv[2 * number + 1, :, :HD]], axis=0)
        dk = jnp.dot(slope, q_s[...], preferred_element_type=F32)
        dv = jnp.dot(probs, g_s[...], preferred_element_type=F32)
        grads = jnp.concatenate([dk, dv], axis=1).astype(BF16)
        for side in range(2):
            index = 2 * number + side
            pb[index] = grads[side * SLOT : (side + 1) * SLOT]

            @pl.when(index != mate)
            def _():
                pb_send(index).start()

        dqt_s[...] += tn(keys, slope)
        return carry

    lax.fori_loop(0, run + 1, grad_step, 0)
    rb[mate] = pb[mate]

    turned = dqt_s[...].T.astype(BF16)
    for number in range(GROUP):
        cols = slice(number * HD, (number + 1) * HD)
        dqs[:, :, cols] = turned[number * SLOT : (number + 1) * SLOT].reshape(QUAD, ROWS, HD)

    def dq_copy(step):
        to = other(step)
        return remote(dqs.at[to], dqr.at[head], dq_ss.at[step], dq_rs.at[step], quad_at(to))

    for step in range(1, QUAD):
        dq_copy(step).start()
    dqr[head] = dqs[head]

    for step in range(1, QUAD):
        t_copy(step).wait_recv()
    term = tr[0, 0:1] + tr[1, 0:1] + tr[2, 0:1] + tr[3, 0:1]
    spot = lax.broadcasted_iota(jnp.int32, (ROWS, SLOT), 0) + head * ROWS
    pick = lax.broadcasted_iota(jnp.int32, (ROWS, SLOT), 1) == spot
    term = jnp.sum(jnp.where(pick, jnp.broadcast_to(term, (ROWS, SLOT)), 0.0), axis=1, keepdims=True)
    logit_grad = (1.0 - gate_s[:, 0:1]) * term
    part = jnp.sum(logit_grad * x_ref[...].astype(F32), axis=0, keepdims=True)
    for number in range(32):
        rp[number : number + 1, :] = part[:, number * 128 : (number + 1) * 128]

    def r1_copy(step):
        to = other(step)
        return remote(
            rp.at[pl.ds(pl.multiple_of(to * 8, 8), 8)], r1.at[head], r1_ss.at[step], r1_rs.at[step], quad_at(to)
        )

    for step in range(1, QUAD):
        r1_copy(step).start()
    r1[head] = rp[pl.ds(pl.multiple_of(head * 8, 8), 8)]
    for step in range(1, QUAD):
        r1_copy(step).wait_recv()
    r2s[...] = r1[0] + r1[1] + r1[2] + r1[3]

    def r2_send(index):
        return remote(r2s, r2.at[mate], r2_ss.at[index], r2_rs.at[mate], mate_at(index))

    def r2_recv(index):
        return remote(r2s, r2.at[index], r2_ss.at[index], r2_rs.at[index], mate_at(index))

    def r2_start(index, carry):
        @pl.when(index != mate)
        def _():
            r2_send(index).start()

        return carry

    lax.fori_loop(0, MATES, r2_start, 0)
    r2[mate] = r2s[...]

    def gather_sum(index, total):
        @pl.when(index != mate)
        def _():
            pb_recv(index).wait_recv()

        return total + rb[index].astype(F32)

    total = lax.fori_loop(run * 2, MATES, gather_sum, jnp.zeros((SLOT, 2 * HD), F32))
    cb[...] = total.astype(BF16)

    def kr_copy(step):
        to = other(step)
        return remote(
            cb.at[pl.ds(pl.multiple_of(to * ROWS, ROWS), ROWS)], kr.at[head], kr_ss.at[step], kr_rs.at[step],
            quad_at(to),
        )

    for step in range(1, QUAD):
        kr_copy(step).start()
    kr[head] = cb[pl.ds(pl.multiple_of(head * ROWS, ROWS), ROWS)]

    def r2_sum(index, total):
        @pl.when(index != mate)
        def _():
            r2_recv(index).wait_recv()

        return total + r2[index]

    r3s[...] = lax.fori_loop(0, MATES, r2_sum, jnp.zeros((8, 128), F32))

    def r3_copy(step):
        return remote(r3s, r3.at[dp], r3_ss.at[step], r3_rs.at[step], dp_at(other_dp(step)))

    for step in range(1, 4):
        r3_copy(step).start()
    r3[dp] = r3s[...]

    back_cos = cos_s[...]
    back_sin = sin_s[...]

    def turn_back(rows):
        return rows * back_cos - pltpu.roll(rows, HD // 2, 1) * back_sin

    for step in range(1, QUAD):
        dq_copy(step).wait_recv()
    for number in range(HQ):
        cols = slice((number % GROUP) * HD, (number % GROUP + 1) * HD)
        rows = dqr[number // GROUP, :, cols].astype(F32)
        dq_out[:, number * HD : (number + 1) * HD] = turn_back(rows).astype(BF16)

    for step in range(1, 4):
        r3_copy(step).wait_recv()
    own = pl.ds(pl.multiple_of(head * 8, 8), 8)
    r4[own] = (r3[0] + r3[1] + r3[2] + r3[3]) * (1.0 / math.sqrt(4 * 2048))

    def r4_copy(step):
        return remote(r4.at[own], r4.at[own], r4_ss.at[step], r4_rs.at[step], quad_at(other(step)))

    for step in range(1, QUAD):
        r4_copy(step).start()

    for step in range(1, QUAD):
        kr_copy(step).wait_recv()
    for number in range(KVH):
        cols = slice(number * HD, (number + 1) * HD)
        dk_out[:, cols] = turn_back(kr[number, :, :HD].astype(F32)).astype(BF16)
        dv_out[:, cols] = kr[number, :, HD:]

    for step in range(1, QUAD):
        r4_copy(step).wait_recv()
    r_out[...] = r4[...]

    for step in range(1, QUAD):
        for copy in (kv_copy, qg_copy, t_copy, dq_copy, r1_copy, kr_copy, r3_copy, r4_copy):
            copy(step).wait_send()

    def drain_late(index, carry):
        @pl.when(index != mate)
        def _():
            ga_send(index).wait_send()

        return carry

    lax.fori_loop(run * 2, MATES, drain_late, 0)

    def drain_early(index, carry):
        @pl.when(index != mate)
        def _():
            pb_send(index).wait_send()

        return carry

    lax.fori_loop(0, run * 2 + 2, drain_early, 0)

    def drain_all(index, carry):
        @pl.when(index != mate)
        def _():
            r2_send(index).wait_send()

        return carry

    lax.fori_loop(0, MATES, drain_all, 0)


def shards(queries, keys, values, out_grad, routed_inputs, router_weight, positions):
    vmem = pl.BlockSpec(memory_space=pltpu.VMEM)
    dma = pltpu.SemaphoreType.DMA
    scratch = [
        pltpu.VMEM((ROWS, HD), F32),
        pltpu.VMEM((ROWS, HD), F32),
        pltpu.VMEM((ROWS, HD), F32),
        pltpu.VMEM((KVH, ROWS, 2 * HD), BF16),
        pltpu.VMEM((QUAD, 2, ROWS, GROUP * HD), BF16),
        pltpu.VMEM((MATES, SLOT, 2 * HD), BF16),
        pltpu.VMEM((QUAD, 2, ROWS, GROUP * HD), BF16),
        pltpu.VMEM((QROWS, HD), BF16),
        pltpu.VMEM((QROWS, HD), BF16),
        pltpu.VMEM((SUPER, SPAN, QROWS), F32),
        pltpu.VMEM((SUPER, SPAN, QROWS), F32),
        pltpu.VMEM((HD, QROWS), F32),
        pltpu.VMEM((MATES, SLOT, 2 * HD), BF16),
        pltpu.VMEM((MATES, SLOT, 2 * HD), BF16),
        pltpu.VMEM((QUAD, ROWS, GROUP * HD), BF16),
        pltpu.VMEM((QUAD, ROWS, GROUP * HD), BF16),
        pltpu.VMEM((SLOT, 2 * HD), BF16),
        pltpu.VMEM((QUAD, ROWS, 2 * HD), BF16),
        pltpu.VMEM((8, 128), F32),
        pltpu.VMEM((QUAD, 8, 128), F32),
        pltpu.VMEM((32, 128), F32),
        pltpu.VMEM((QUAD, 8, 128), F32),
        pltpu.VMEM((8, 128), F32),
        pltpu.VMEM((MATES, 8, 128), F32),
        pltpu.VMEM((8, 128), F32),
        pltpu.VMEM((4, 8, 128), F32),
        pltpu.VMEM((32, 128), F32),
        dma((QUAD,)), dma((QUAD,)), dma((QUAD,)), dma((QUAD,)),
        dma((MATES,)), dma((MATES,)), dma((MATES,)), dma((MATES,)),
        dma((QUAD,)), dma((QUAD,)), dma((QUAD,)), dma((QUAD,)),
        dma((QUAD,)), dma((QUAD,)), dma((QUAD,)), dma((QUAD,)),
        dma((MATES,)), dma((MATES,)), dma((QUAD,)), dma((QUAD,)),
        dma((QUAD,)), dma((QUAD,)),
    ]
    query_grad, key_grad, value_grad, router = pl.pallas_call(
        kernel,
        out_shape=(
            jax.ShapeDtypeStruct((ROWS, HQ * HD), BF16),
            jax.ShapeDtypeStruct((ROWS, KVH * HD), BF16),
            jax.ShapeDtypeStruct((ROWS, KVH * HD), BF16),
            jax.ShapeDtypeStruct((32, 128), F32),
        ),
        in_specs=[vmem] * 8,
        out_specs=(vmem,) * 4,
        scratch_shapes=scratch,
        compiler_params=pltpu.CompilerParams(
            collective_id=0, has_side_effects=True, vmem_limit_bytes=40 * 1024 * 1024
        ),
    )(
        queries[0],
        keys[0],
        values[0],
        out_grad[0],
        routed_inputs[0],
        router_weight.reshape(1, -1),
        positions,
        jnp.asarray(rope_rows()),
    )
    return (query_grad[None], key_grad[None], value_grad[None], router.reshape(-1))


def solution(mesh):
    row = P("dp", "ctx", None)
    in_specs = (row, row, row, row, row, P(), P("dp", "ctx"))
    out_specs = (row, row, row, P())
    return jax.shard_map(shards, mesh=mesh, in_specs=in_specs, out_specs=out_specs, check_vma=False)
```

```python
import math

import jax
import jax.numpy as jnp
import numpy as np
from jax import lax
from jax.experimental import pallas as pl
from jax.experimental.pallas import tpu as pltpu
from jax.sharding import PartitionSpec as P

HQ = 16
KVH = 4
HD = 128
ROPE_BASE = 500000.0
SCORE_SCALE = 1.0 / math.sqrt(HD)
MESH = pl.DeviceIdType.MESH

ROWS = 32
QUAD = 4
MATES = 16
SUPER = 8
SLOT = QUAD * ROWS
SPAN = 2 * SLOT
GROUP = HQ // KVH
QROWS = GROUP * SLOT
NEG = -1e30
F32 = jnp.float32
BF16 = jnp.bfloat16


def rope_rows():
    pairs = HD // 2
    frequency = [ROPE_BASE ** (-number / pairs) for number in range(pairs)]
    coarse = [256.0 * factor % (2.0 * math.pi) for factor in frequency]
    table = np.zeros((8, HD), np.float32)
    table[0] = np.asarray(frequency + frequency, np.float32)
    table[1] = np.asarray(coarse + coarse, np.float32)
    return table


def nt(left, right):
    return lax.dot_general(left, right, (((1,), (1,)), ((), ())), preferred_element_type=F32)


def tn(left, right):
    return lax.dot_general(left, right, (((0,), (0,)), ((), ())), preferred_element_type=F32)


def kernel(
    q_hbm, k_hbm, v_hbm, g_hbm, x_hbm, w_hbm, p_hbm, rope_hbm,
    dqr, kr, cos_s, sin_s, r4,
    q_ref, k_ref, v_ref, g_ref, x_ref, w_ref, p_ref, rope_ref, in_sem, gate_s, kv4, qg4, kv, qg, q_s, g_s, s_s, d_s, dqt_s, pb, rb, dqs, cb,
    ts, tr, rp, r1, r2s, r2, r3s, r3,
    kv_ss, kv_rs, qg_ss, qg_rs, ga_ss, ga_rs, pb_ss, pb_rs, dq_ss, dq_rs, kr_ss, kr_rs,
    t_ss, t_rs, r1_ss, r1_rs, r2_ss, r2_rs, r3_ss, r3_rs, r4_ss, r4_rs,
):
    dp = lax.axis_index("dp")
    ctx = lax.axis_index("ctx")
    run = ctx // 8
    z = ctx % 8
    head = z // 2
    par = z % 2
    mate = run * 2 + par

    def quad_at(member):
        return (dp, run * 8 + 2 * member + par)

    def mate_at(index):
        return (dp, (index // 2) * 8 + 2 * head + index % 2)

    def dp_at(index):
        return (index, ctx)

    def remote(src, dst, send, recv, to):
        return pltpu.make_async_remote_copy(
            src_ref=src, dst_ref=dst, send_sem=send, recv_sem=recv, device_id=to, device_id_type=MESH
        )

    def other(step):
        return lax.rem(head + step, QUAD)

    def other_dp(step):
        return lax.rem(dp + step, 4)

    barrier = pltpu.get_barrier_semaphore()
    for step in range(1, QUAD):
        pl.semaphore_signal(barrier, inc=1, device_id=quad_at(other(step)), device_id_type=MESH)
        pl.semaphore_signal(barrier, inc=1, device_id=dp_at(other_dp(step)), device_id_type=MESH)

    def greet(step, carry):
        pl.semaphore_signal(
            barrier, inc=1, device_id=mate_at(lax.rem(mate + step, MATES)), device_id_type=MESH
        )
        return carry

    lax.fori_loop(1, MATES, greet, 0)

    pairs = (
        (p_hbm, p_ref), (rope_hbm, rope_ref), (k_hbm, k_ref), (v_hbm, v_ref),
        (x_hbm, x_ref), (w_hbm, w_ref), (q_hbm, q_ref), (g_hbm, g_ref),
    )
    fetches = [
        pltpu.make_async_copy(src, dst, in_sem.at[number]) for number, (src, dst) in enumerate(pairs)
    ]
    for fetch in fetches:
        fetch.start()
    fetches[0].wait()
    fetches[1].wait()

    eye = lax.broadcasted_iota(jnp.int32, (ROWS, ROWS), 0) == lax.broadcasted_iota(
        jnp.int32, (ROWS, ROWS), 1
    )
    places = jnp.broadcast_to(p_ref[...], (ROWS, ROWS))
    upper = jnp.sum(jnp.where(eye, (places >> 8).astype(F32), 0.0), axis=1, keepdims=True)
    lower = jnp.sum(jnp.where(eye, (places & 255).astype(F32), 0.0), axis=1, keepdims=True)
    angles = upper * rope_ref[1:2, :] + lower * rope_ref[0:1, :]
    lane = lax.broadcasted_iota(jnp.int32, (ROWS, HD), 1)
    cos = jnp.cos(angles)
    sin = jnp.sin(angles)
    sin = jnp.where(lane < HD // 2, -sin, sin)
    cos_s[...] = cos
    sin_s[...] = sin

    def turn(rows):
        return rows * cos + pltpu.roll(rows, HD // 2, 1) * sin

    fetches[2].wait()
    fetches[3].wait()
    for number in range(KVH):
        cols = slice(number * HD, (number + 1) * HD)
        kv4[number, :, :HD] = turn(k_ref[:, cols].astype(F32)).astype(BF16)
        kv4[number, :, HD:] = v_ref[:, cols]

    pl.semaphore_wait(barrier, 2 * (QUAD - 1) + MATES - 1)

    def kv_copy(step):
        to = other(step)
        return remote(
            kv4.at[to], kv.at[mate, pl.ds(head * ROWS, ROWS)], kv_ss.at[step], kv_rs.at[step], quad_at(to)
        )

    for step in range(1, QUAD):
        kv_copy(step).start()
    kv[mate, pl.ds(pl.multiple_of(head * ROWS, ROWS), ROWS)] = kv4[head]

    for fetch in fetches[4:]:
        fetch.wait()
    logits = jnp.sum(x_ref[...].astype(F32) * w_ref[...], axis=1, keepdims=True)
    gate = jax.nn.sigmoid(logits)
    gate_s[...] = jnp.broadcast_to(gate, (ROWS, HD))
    for number in range(HQ):
        cols = slice(number * HD, (number + 1) * HD)
        part, into = number // GROUP, slice((number % GROUP) * HD, (number % GROUP + 1) * HD)
        qg4[part, 0, :, into] = turn(q_ref[:, cols].astype(F32)).astype(BF16)
        qg4[part, 1, :, into] = (gate * g_ref[:, cols].astype(F32)).astype(BF16)

    def qg_copy(step):
        to = other(step)
        return remote(qg4.at[to], qg.at[head], qg_ss.at[step], qg_rs.at[step], quad_at(to))

    for step in range(1, QUAD):
        qg_copy(step).start()
    qg[head] = qg4[head]

    for step in range(1, QUAD):
        kv_copy(step).wait_recv()

    def ga_send(index):
        return remote(kv.at[mate], kv.at[mate], ga_ss.at[index], ga_rs.at[mate], mate_at(index))

    def ga_recv(index):
        return remote(kv.at[mate], kv.at[index], ga_ss.at[index], ga_rs.at[index], mate_at(index))

    def ga_start(index, carry):
        @pl.when(index != mate)
        def _():
            ga_send(index).start()

        return carry

    lax.fori_loop(run * 2, MATES, ga_start, 0)

    for step in range(1, QUAD):
        qg_copy(step).wait_recv()
    for number in range(GROUP):
        cols = slice(number * HD, (number + 1) * HD)
        q_s[number * SLOT : (number + 1) * SLOT, :] = qg[:, 0, :, cols].reshape(SLOT, HD)
        g_s[number * SLOT : (number + 1) * SLOT, :] = qg[:, 1, :, cols].reshape(SLOT, HD)

    key_at = lax.broadcasted_iota(jnp.int32, (SPAN, QROWS), 0)
    key_at = (key_at >> 7) * ROWS + ((key_at & 96) << 1) + (key_at & 31)
    row_at = lax.broadcasted_iota(jnp.int32, (SPAN, QROWS), 1)
    row_at = par * ROWS + ((row_at & 96) << 1) + (row_at & 31)
    ahead = key_at - row_at

    def score_step(back, top):
        number = run - back
        for side in range(2):
            index = 2 * number + side

            @pl.when(index != mate)
            def _():
                ga_recv(index).wait_recv()

        both = jnp.concatenate([kv[2 * number], kv[2 * number + 1]], axis=0)
        scores = nt(both[:, :HD], q_s[...]) * (SCORE_SCALE * math.log2(math.e))
        scores = jnp.where(ahead <= (run - number) * SPAN, scores, NEG)
        s_s[number] = scores
        d_s[number] = nt(both[:, HD:], g_s[...]) * SCORE_SCALE
        return jnp.maximum(top, jnp.max(scores, axis=0, keepdims=True))

    top = lax.fori_loop(0, run + 1, score_step, jnp.full((1, QROWS), NEG, F32))

    def mass_step(number, carry):
        mass, pull = carry
        raised = jnp.exp2(s_s[number] - top)
        s_s[number] = raised
        return (
            mass + jnp.sum(raised, axis=0, keepdims=True),
            pull + jnp.sum(raised * d_s[number], axis=0, keepdims=True),
        )

    zero_row = jnp.zeros((1, QROWS), F32)
    mass, pull = lax.fori_loop(0, run + 1, mass_step, (zero_row, zero_row))
    inverse = 1.0 / mass
    delta = pull * inverse

    term = delta[:, :SLOT]
    for number in range(1, GROUP):
        term = term + delta[:, number * SLOT : (number + 1) * SLOT]
    ts[...] = jnp.broadcast_to(term * math.sqrt(HD), (8, SLOT))

    def t_copy(step):
        return remote(ts, tr.at[head], t_ss.at[step], t_rs.at[step], quad_at(other(step)))

    for step in range(1, QUAD):
        t_copy(step).start()
    tr[head] = ts[...]

    def pb_send(index):
        return remote(pb.at[index], rb.at[mate], pb_ss.at[index], pb_rs.at[mate], mate_at(index))

    def pb_recv(index):
        return remote(pb.at[index], rb.at[index], pb_ss.at[index], pb_rs.at[index], mate_at(index))

    dqt_s[...] = jnp.zeros_like(dqt_s)

    def grad_step(number, carry):
        weights = s_s[number] * inverse
        probs = weights.astype(BF16)
        slope = (weights * (d_s[number] - delta)).astype(BF16)
        keys = jnp.concatenate([kv[2 * number, :, :HD], kv[2 * number + 1, :, :HD]], axis=0)
        dk = jnp.dot(slope, q_s[...], preferred_element_type=F32)
        dv = jnp.dot(probs, g_s[...], preferred_element_type=F32)
        grads = jnp.concatenate([dk, dv], axis=1).astype(BF16)
        for side in range(2):
            index = 2 * number + side
            pb[index] = grads[side * SLOT : (side + 1) * SLOT]

            @pl.when(index != mate)
            def _():
                pb_send(index).start()

        dqt_s[...] += tn(keys, slope)
        return carry

    half = (run + 1) // 2
    lax.fori_loop(0, half, grad_step, 0)

    for step in range(1, QUAD):
        t_copy(step).wait_recv()
    term = tr[0] + tr[1] + tr[2] + tr[3]
    spot = lax.broadcasted_iota(jnp.int32, (ROWS, SLOT), 0) + head * ROWS
    pick = lax.broadcasted_iota(jnp.int32, (ROWS, SLOT), 1) == spot
    term = jnp.concatenate([term] * (ROWS // 8), axis=0)
    term = jnp.sum(jnp.where(pick, term, 0.0), axis=1, keepdims=True)
    logit_grad = (1.0 - gate_s[:, 0:1]) * term
    part = jnp.sum(logit_grad * x_ref[...].astype(F32), axis=0, keepdims=True)
    for number in range(32):
        rp[number : number + 1, :] = part[:, number * 128 : (number + 1) * 128]

    own = pl.ds(pl.multiple_of(head * 8, 8), 8)

    def r1_copy(step):
        to = other(step)
        rows = pl.ds(pl.multiple_of(to * 8, 8), 8)
        return remote(rp.at[rows], r1.at[head], r1_ss.at[step], r1_rs.at[step], quad_at(to))

    for step in range(1, QUAD):
        r1_copy(step).start()
    r1[head] = rp[own]

    lax.fori_loop(half, run + 1, grad_step, 0)

    for step in range(1, QUAD):
        r1_copy(step).wait_recv()
    r2s[...] = r1[0] + r1[1] + r1[2] + r1[3]

    def r2_send(index):
        return remote(r2s, r2.at[mate], r2_ss.at[index], r2_rs.at[mate], mate_at(index))

    def r2_recv(index):
        return remote(r2s, r2.at[index], r2_ss.at[index], r2_rs.at[index], mate_at(index))

    def r2_start(index, carry):
        @pl.when(index != mate)
        def _():
            r2_send(index).start()

        return carry

    lax.fori_loop(0, MATES, r2_start, 0)
    r2[mate] = r2s[...]

    turned = dqt_s[...].T.astype(BF16)
    for number in range(GROUP):
        cols = slice(number * HD, (number + 1) * HD)
        dqs[:, :, cols] = turned[number * SLOT : (number + 1) * SLOT].reshape(QUAD, ROWS, HD)

    def dq_copy(step):
        to = other(step)
        return remote(dqs.at[to], dqr.at[head], dq_ss.at[step], dq_rs.at[step], quad_at(to))

    for step in range(1, QUAD):
        dq_copy(step).start()
    dqr[head] = dqs[head]

    rb[mate] = pb[mate]

    def gather_sum(index, total):
        @pl.when(index != mate)
        def _():
            pb_recv(index).wait_recv()

        return total + rb[index].astype(F32)

    middle = run + MATES // 2
    total = lax.fori_loop(run * 2, middle, gather_sum, jnp.zeros((SLOT, 2 * HD), F32))

    def r2_sum(index, total):
        @pl.when(index != mate)
        def _():
            r2_recv(index).wait_recv()

        return total + r2[index]

    r3s[...] = lax.fori_loop(0, MATES, r2_sum, jnp.zeros((8, 128), F32))

    def r3_copy(step):
        return remote(r3s, r3.at[dp], r3_ss.at[step], r3_rs.at[step], dp_at(other_dp(step)))

    for step in range(1, 4):
        r3_copy(step).start()
    r3[dp] = r3s[...]

    total = lax.fori_loop(middle, MATES, gather_sum, total)
    cb[...] = total.astype(BF16)

    def kr_copy(step):
        to = other(step)
        rows = pl.ds(pl.multiple_of(to * ROWS, ROWS), ROWS)
        return remote(cb.at[rows], kr.at[head], kr_ss.at[step], kr_rs.at[step], quad_at(to))

    for step in range(1, QUAD):
        kr_copy(step).start()
    kr[head] = cb[pl.ds(pl.multiple_of(head * ROWS, ROWS), ROWS)]

    for step in range(1, 4):
        r3_copy(step).wait_recv()
    r4[own] = (r3[0] + r3[1] + r3[2] + r3[3]) * (1.0 / math.sqrt(4 * 2048))

    def r4_copy(step):
        return remote(r4.at[own], r4.at[own], r4_ss.at[step], r4_rs.at[step], quad_at(other(step)))

    for step in range(1, QUAD):
        r4_copy(step).start()

    for step in range(1, QUAD):
        for copy in (kv_copy, qg_copy, t_copy, dq_copy, r1_copy, r3_copy):
            copy(step).wait_send()

    def drain_late(index, carry):
        @pl.when(index != mate)
        def _():
            ga_send(index).wait_send()

        return carry

    lax.fori_loop(run * 2, MATES, drain_late, 0)

    def drain_early(index, carry):
        @pl.when(index != mate)
        def _():
            pb_send(index).wait_send()

        return carry

    lax.fori_loop(0, run * 2 + 2, drain_early, 0)

    def drain_all(index, carry):
        @pl.when(index != mate)
        def _():
            r2_send(index).wait_send()

        return carry

    lax.fori_loop(0, MATES, drain_all, 0)
    for step in range(1, QUAD):
        for copy in (dq_copy, kr_copy, r4_copy):
            copy(step).wait_recv()
        for copy in (kr_copy, r4_copy):
            copy(step).wait_send()


def finish(dqr, kr, cos_s, sin_s, r4, dq_out, dk_out, dv_out, r_out):
    cos = cos_s[...]
    sin = sin_s[...]

    def turn_back(rows):
        return rows * cos - pltpu.roll(rows, HD // 2, 1) * sin

    for number in range(HQ):
        cols = slice((number % GROUP) * HD, (number % GROUP + 1) * HD)
        rows = dqr[number // GROUP, :, cols].astype(F32)
        dq_out[:, number * HD : (number + 1) * HD] = turn_back(rows).astype(BF16)
    for number in range(KVH):
        cols = slice(number * HD, (number + 1) * HD)
        dk_out[:, cols] = turn_back(kr[number, :, :HD].astype(F32)).astype(BF16)
        dv_out[:, cols] = kr[number, :, HD:]
    r_out[...] = r4[...]


def shards(queries, keys, values, out_grad, routed_inputs, router_weight, positions):
    vmem = pl.BlockSpec(memory_space=pltpu.VMEM)
    hbm = pl.BlockSpec(memory_space=pltpu.HBM)
    dma = pltpu.SemaphoreType.DMA
    scratch = [
        pltpu.VMEM((ROWS, HQ * HD), BF16),
        pltpu.VMEM((ROWS, KVH * HD), BF16),
        pltpu.VMEM((ROWS, KVH * HD), BF16),
        pltpu.VMEM((ROWS, HQ * HD), BF16),
        pltpu.VMEM((ROWS, 4096), BF16),
        pltpu.VMEM((1, 4096), F32),
        pltpu.VMEM((1, ROWS), jnp.int32),
        pltpu.VMEM((8, HD), F32),
        dma((8,)),
        pltpu.VMEM((ROWS, HD), F32),
        pltpu.VMEM((KVH, ROWS, 2 * HD), BF16),
        pltpu.VMEM((QUAD, 2, ROWS, GROUP * HD), BF16),
        pltpu.VMEM((MATES, SLOT, 2 * HD), BF16),
        pltpu.VMEM((QUAD, 2, ROWS, GROUP * HD), BF16),
        pltpu.VMEM((QROWS, HD), BF16),
        pltpu.VMEM((QROWS, HD), BF16),
        pltpu.VMEM((SUPER, SPAN, QROWS), F32),
        pltpu.VMEM((SUPER, SPAN, QROWS), F32),
        pltpu.VMEM((HD, QROWS), F32),
        pltpu.VMEM((MATES, SLOT, 2 * HD), BF16),
        pltpu.VMEM((MATES, SLOT, 2 * HD), BF16),
        pltpu.VMEM((QUAD, ROWS, GROUP * HD), BF16),
        pltpu.VMEM((SLOT, 2 * HD), BF16),
        pltpu.VMEM((8, 128), F32),
        pltpu.VMEM((QUAD, 8, 128), F32),
        pltpu.VMEM((32, 128), F32),
        pltpu.VMEM((QUAD, 8, 128), F32),
        pltpu.VMEM((8, 128), F32),
        pltpu.VMEM((MATES, 8, 128), F32),
        pltpu.VMEM((8, 128), F32),
        pltpu.VMEM((4, 8, 128), F32),
        dma((QUAD,)), dma((QUAD,)), dma((QUAD,)), dma((QUAD,)),
        dma((MATES,)), dma((MATES,)), dma((MATES,)), dma((MATES,)),
        dma((QUAD,)), dma((QUAD,)), dma((QUAD,)), dma((QUAD,)),
        dma((QUAD,)), dma((QUAD,)), dma((QUAD,)), dma((QUAD,)),
        dma((MATES,)), dma((MATES,)), dma((QUAD,)), dma((QUAD,)),
        dma((QUAD,)), dma((QUAD,)),
    ]
    landed = pl.pallas_call(
        kernel,
        out_shape=(
            jax.ShapeDtypeStruct((QUAD, ROWS, GROUP * HD), BF16),
            jax.ShapeDtypeStruct((QUAD, ROWS, 2 * HD), BF16),
            jax.ShapeDtypeStruct((ROWS, HD), F32),
            jax.ShapeDtypeStruct((ROWS, HD), F32),
            jax.ShapeDtypeStruct((32, 128), F32),
        ),
        in_specs=[hbm] * 8,
        out_specs=(vmem,) * 5,
        scratch_shapes=scratch,
        compiler_params=pltpu.CompilerParams(
            collective_id=0, has_side_effects=True, vmem_limit_bytes=63 * 1024 * 1024
        ),
    )(
        queries[0],
        keys[0],
        values[0],
        out_grad[0],
        routed_inputs[0],
        router_weight.reshape(1, -1),
        positions,
        jnp.asarray(rope_rows()),
    )
    query_grad, key_grad, value_grad, router = pl.pallas_call(
        finish,
        out_shape=(
            jax.ShapeDtypeStruct((ROWS, HQ * HD), BF16),
            jax.ShapeDtypeStruct((ROWS, KVH * HD), BF16),
            jax.ShapeDtypeStruct((ROWS, KVH * HD), BF16),
            jax.ShapeDtypeStruct((32, 128), F32),
        ),
        in_specs=[vmem] * 5,
        out_specs=(vmem,) * 4,
    )(*landed)
    return (query_grad[None], key_grad[None], value_grad[None], router.reshape(-1))


def solution(mesh):
    row = P("dp", "ctx", None)
    in_specs = (row, row, row, row, row, P(), P("dp", "ctx"))
    out_specs = (row, row, row, P())
    return jax.shard_map(shards, mesh=mesh, in_specs=in_specs, out_specs=out_specs, check_vma=False)
```

```python
import math

import jax
import jax.numpy as jnp
import numpy as np
from jax import lax
from jax.experimental import pallas as pl
from jax.experimental.pallas import tpu as pltpu
from jax.sharding import PartitionSpec as P

HQ = 16
KVH = 4
HD = 128
ROPE_BASE = 500000.0
SCORE_SCALE = 1.0 / math.sqrt(HD)
MESH = pl.DeviceIdType.MESH

ROWS = 32
QUAD = 4
MATES = 16
SUPER = 8
SLOT = QUAD * ROWS
SPAN = 2 * SLOT
GROUP = HQ // KVH
QROWS = GROUP * SLOT
NEG = -1e30
F32 = jnp.float32
BF16 = jnp.bfloat16


def rope_rows():
    pairs = HD // 2
    frequency = [ROPE_BASE ** (-number / pairs) for number in range(pairs)]
    coarse = [256.0 * factor % (2.0 * math.pi) for factor in frequency]
    table = np.zeros((8, HD), np.float32)
    table[0] = np.asarray(frequency + frequency, np.float32)
    table[1] = np.asarray(coarse + coarse, np.float32)
    return table


def nt(left, right):
    return lax.dot_general(left, right, (((1,), (1,)), ((), ())), preferred_element_type=F32)


def tn(left, right):
    return lax.dot_general(left, right, (((0,), (0,)), ((), ())), preferred_element_type=F32)


def kernel(
    q_hbm, k_hbm, v_hbm, g_hbm, x_hbm, w_hbm, p_hbm, rope_hbm,
    dqr, kr, cos_s, sin_s, r_sum,
    q_ref, k_ref, v_ref, g_ref, x_ref, w_ref, p_ref, rope_ref, in_sem, gate_s, kv4, qg4, kv, qg, q_s, g_s, s_s, d_s, dqt_s, pb, rb, dqs, cb,
    ts, tr, rz_s, rz, ry_s, ry, rx_s, rx,
    kv_ss, kv_rs, qg_ss, qg_rs, ga_ss, ga_rs, pb_ss, pb_rs, dq_ss, dq_rs, kr_ss, kr_rs,
    t_ss, t_rs, rz_ss, rz_rs, ry_ss, ry_rs, rx_ss, rx_rs,
):
    dp = lax.axis_index("dp")
    ctx = lax.axis_index("ctx")
    run = ctx // 8
    z = ctx % 8
    head = z // 2
    par = z % 2
    mate = run * 2 + par
    row = run // 2
    side_x = dp * 2 + run % 2

    def quad_at(member):
        return (dp, run * 8 + 2 * member + par)

    def mate_at(index):
        return (dp, (index // 2) * 8 + 2 * head + index % 2)

    def z_at(step):
        return (dp, run * 8 + lax.rem(z + step, 8))

    def y_at(step):
        return (dp, lax.rem(ctx + 16 * step, 64))

    def x_at(step):
        to = lax.rem(side_x + step, 8)
        return (to // 2, (row * 2 + to % 2) * 8 + z)

    def remote(src, dst, send, recv, to):
        return pltpu.make_async_remote_copy(
            src_ref=src, dst_ref=dst, send_sem=send, recv_sem=recv, device_id=to, device_id_type=MESH
        )

    def other(step):
        return lax.rem(head + step, QUAD)

    barrier = pltpu.get_barrier_semaphore()

    def greet_near(step, carry):
        pl.semaphore_signal(barrier, inc=1, device_id=z_at(step), device_id_type=MESH)
        pl.semaphore_signal(barrier, inc=1, device_id=x_at(step), device_id_type=MESH)
        return carry

    lax.fori_loop(1, 8, greet_near, 0)

    def greet(step, carry):
        pl.semaphore_signal(
            barrier, inc=1, device_id=mate_at(lax.rem(mate + step, MATES)), device_id_type=MESH
        )
        return carry

    lax.fori_loop(1, MATES, greet, 0)

    pairs = (
        (p_hbm, p_ref), (rope_hbm, rope_ref), (k_hbm, k_ref), (v_hbm, v_ref),
        (x_hbm, x_ref), (w_hbm, w_ref), (q_hbm, q_ref), (g_hbm, g_ref),
    )
    fetches = [
        pltpu.make_async_copy(src, dst, in_sem.at[number]) for number, (src, dst) in enumerate(pairs)
    ]
    for fetch in fetches:
        fetch.start()
    fetches[0].wait()
    fetches[1].wait()

    eye = lax.broadcasted_iota(jnp.int32, (ROWS, ROWS), 0) == lax.broadcasted_iota(
        jnp.int32, (ROWS, ROWS), 1
    )
    places = jnp.broadcast_to(p_ref[...], (ROWS, ROWS))
    upper = jnp.sum(jnp.where(eye, (places >> 8).astype(F32), 0.0), axis=1, keepdims=True)
    lower = jnp.sum(jnp.where(eye, (places & 255).astype(F32), 0.0), axis=1, keepdims=True)
    angles = upper * rope_ref[1:2, :] + lower * rope_ref[0:1, :]
    lane = lax.broadcasted_iota(jnp.int32, (ROWS, HD), 1)
    cos = jnp.cos(angles)
    sin = jnp.sin(angles)
    sin = jnp.where(lane < HD // 2, -sin, sin)
    cos_s[...] = cos
    sin_s[...] = sin

    def turn(rows):
        return rows * cos + pltpu.roll(rows, HD // 2, 1) * sin

    fetches[2].wait()
    fetches[3].wait()
    for number in range(KVH):
        cols = slice(number * HD, (number + 1) * HD)
        kv4[number, :, :HD] = turn(k_ref[:, cols].astype(F32)).astype(BF16)
        kv4[number, :, HD:] = v_ref[:, cols]

    pl.semaphore_wait(barrier, 2 * 7 + MATES - 1)

    def kv_copy(step):
        to = other(step)
        rows = pl.ds((QUAD - step) * ROWS, ROWS)
        return remote(kv4.at[to], kv.at[mate, rows], kv_ss.at[step], kv_rs.at[step], quad_at(to))

    def ga_send(part, index):
        rows = kv.at[mate, pl.ds(part * ROWS, ROWS if part == 0 else 3 * ROWS)]
        return remote(rows, rows, ga_ss.at[part, index], ga_rs.at[part, mate], mate_at(index))

    def ga_recv(part, index):
        rows = kv.at[index, pl.ds(part * ROWS, ROWS if part == 0 else 3 * ROWS)]
        return remote(rows, rows, ga_ss.at[part, index], ga_rs.at[part, index], mate_at(index))

    def ga_start(part):
        def start(step, carry):
            index = run * 2 + MATES - 1 - step

            @pl.when(index != mate)
            def _():
                ga_send(part, index).start()

            return carry

        lax.fori_loop(run * 2, MATES, start, 0)

    for step in range(1, QUAD):
        kv_copy(step).start()
    kv[mate, :ROWS] = kv4[head]
    ga_start(0)

    for fetch in fetches[4:]:
        fetch.wait()
    logits = jnp.sum(x_ref[...].astype(F32) * w_ref[...], axis=1, keepdims=True)
    gate = jax.nn.sigmoid(logits)
    gate_s[...] = jnp.broadcast_to(gate, (ROWS, HD))
    for number in range(HQ):
        cols = slice(number * HD, (number + 1) * HD)
        part, into = number // GROUP, slice((number % GROUP) * HD, (number % GROUP + 1) * HD)
        qg4[part, 0, :, into] = turn(q_ref[:, cols].astype(F32)).astype(BF16)
        qg4[part, 1, :, into] = (gate * g_ref[:, cols].astype(F32)).astype(BF16)

    def qg_copy(step):
        to = other(step)
        return remote(qg4.at[to], qg.at[head], qg_ss.at[step], qg_rs.at[step], quad_at(to))

    for step in range(1, QUAD):
        qg_copy(step).start()
    qg[head] = qg4[head]

    for step in range(1, QUAD):
        kv_copy(step).wait_recv()
    ga_start(1)

    for step in range(1, QUAD):
        qg_copy(step).wait_recv()
    for number in range(GROUP):
        cols = slice(number * HD, (number + 1) * HD)
        q_s[number * SLOT : (number + 1) * SLOT, :] = qg[:, 0, :, cols].reshape(SLOT, HD)
        g_s[number * SLOT : (number + 1) * SLOT, :] = qg[:, 1, :, cols].reshape(SLOT, HD)

    key_at = lax.broadcasted_iota(jnp.int32, (SPAN, QROWS), 0)
    key_at = (key_at >> 7) * ROWS + (((key_at + head * ROWS) & 96) << 1) + (key_at & 31)
    row_at = lax.broadcasted_iota(jnp.int32, (SPAN, QROWS), 1)
    row_at = par * ROWS + ((row_at & 96) << 1) + (row_at & 31)
    ahead = key_at - row_at

    def score_step(back, top):
        number = run - back
        for side in range(2):
            index = 2 * number + side

            @pl.when(index != mate)
            def _():
                for part in range(2):
                    ga_recv(part, index).wait_recv()

        both = jnp.concatenate([kv[2 * number], kv[2 * number + 1]], axis=0)
        scores = nt(both[:, :HD], q_s[...]) * (SCORE_SCALE * math.log2(math.e))
        scores = jnp.where(ahead <= (run - number) * SPAN, scores, NEG)
        s_s[number] = scores
        d_s[number] = nt(both[:, HD:], g_s[...]) * SCORE_SCALE
        return jnp.maximum(top, jnp.max(scores, axis=0, keepdims=True))

    top = lax.fori_loop(0, run + 1, score_step, jnp.full((1, QROWS), NEG, F32))

    def mass_step(number, carry):
        mass, pull = carry
        raised = jnp.exp2(s_s[number] - top)
        s_s[number] = raised
        return (
            mass + jnp.sum(raised, axis=0, keepdims=True),
            pull + jnp.sum(raised * d_s[number], axis=0, keepdims=True),
        )

    zero_row = jnp.zeros((1, QROWS), F32)
    mass, pull = lax.fori_loop(0, run + 1, mass_step, (zero_row, zero_row))
    inverse = 1.0 / mass
    delta = pull * inverse

    term = delta[:, :SLOT]
    for number in range(1, GROUP):
        term = term + delta[:, number * SLOT : (number + 1) * SLOT]
    ts[...] = jnp.broadcast_to(term * math.sqrt(HD), (8, SLOT))

    def t_copy(step):
        return remote(ts, tr.at[head], t_ss.at[step], t_rs.at[step], quad_at(other(step)))

    for step in range(1, QUAD):
        t_copy(step).start()
    tr[head] = ts[...]

    def pb_send(index):
        return remote(pb.at[index], rb.at[mate], pb_ss.at[index], pb_rs.at[mate], mate_at(index))

    def pb_recv(index):
        return remote(pb.at[index], rb.at[index], pb_ss.at[index], pb_rs.at[index], mate_at(index))

    dqt_s[...] = jnp.zeros_like(dqt_s)

    def grad_step(number, carry):
        weights = s_s[number] * inverse
        probs = weights.astype(BF16)
        slope = (weights * (d_s[number] - delta)).astype(BF16)
        keys = jnp.concatenate([kv[2 * number, :, :HD], kv[2 * number + 1, :, :HD]], axis=0)
        dk = jnp.dot(slope, q_s[...], preferred_element_type=F32)
        dv = jnp.dot(probs, g_s[...], preferred_element_type=F32)
        grads = jnp.concatenate([dk, dv], axis=1).astype(BF16)
        for side in range(2):
            index = 2 * number + side
            pb[index] = grads[side * SLOT : (side + 1) * SLOT]

            @pl.when(index != mate)
            def _():
                pb_send(index).start()

        dqt_s[...] += tn(keys, slope)
        return carry

    half = (run + 1) // 2
    lax.fori_loop(0, half, grad_step, 0)

    for step in range(1, QUAD):
        t_copy(step).wait_recv()
    term = tr[0] + tr[1] + tr[2] + tr[3]
    spot = lax.broadcasted_iota(jnp.int32, (ROWS, SLOT), 0) + head * ROWS
    pick = lax.broadcasted_iota(jnp.int32, (ROWS, SLOT), 1) == spot
    term = jnp.concatenate([term] * (ROWS // 8), axis=0)
    term = jnp.sum(jnp.where(pick, term, 0.0), axis=1, keepdims=True)
    logit_grad = (1.0 - gate_s[:, 0:1]) * term
    part = jnp.sum(logit_grad * x_ref[...].astype(F32), axis=0, keepdims=True)
    for number in range(32):
        rz_s[number : number + 1, :] = part[:, number * 128 : (number + 1) * 128]

    def rz_copy(step):
        return remote(rz_s, rz.at[z], rz_ss.at[step], rz_rs.at[step], z_at(step))

    def ry_copy(step):
        return remote(ry_s, ry.at[row], ry_ss.at[step], ry_rs.at[step], y_at(step))

    def rx_copy(step):
        return remote(rx_s, rx.at[side_x], rx_ss.at[step], rx_rs.at[step], x_at(step))

    for step in range(1, 8):
        rz_copy(step).start()
    rz[z] = rz_s[...]

    lax.fori_loop(half, run + 1, grad_step, 0)

    turned = dqt_s[...].T.astype(BF16)
    for number in range(GROUP):
        cols = slice(number * HD, (number + 1) * HD)
        dqs[:, :, cols] = turned[number * SLOT : (number + 1) * SLOT].reshape(QUAD, ROWS, HD)

    def dq_copy(step):
        to = other(step)
        return remote(dqs.at[to], dqr.at[head], dq_ss.at[step], dq_rs.at[step], quad_at(to))

    for step in range(1, QUAD):
        dq_copy(step).start()
    dqr[head] = dqs[head]

    rb[mate] = pb[mate]

    def gather_sum(index, total):
        @pl.when(index != mate)
        def _():
            pb_recv(index).wait_recv()

        return total + rb[index].astype(F32)

    for step in range(1, 8):
        rz_copy(step).wait_recv()
    ry_s[...] = sum((rz[number] for number in range(1, 8)), start=rz[0])
    for step in range(1, 4):
        ry_copy(step).start()
    ry[row] = ry_s[...]

    middle = run + MATES // 2
    total = lax.fori_loop(run * 2, middle, gather_sum, jnp.zeros((SLOT, 2 * HD), F32))

    for step in range(1, 4):
        ry_copy(step).wait_recv()
    rx_s[...] = ry[0] + ry[1] + ry[2] + ry[3]
    for step in range(1, 8):
        rx_copy(step).start()
    rx[side_x] = rx_s[...]

    total = lax.fori_loop(middle, MATES, gather_sum, total)
    cb[...] = total.astype(BF16)

    def kr_copy(step):
        rows = cb.at[pl.ds(step * ROWS, ROWS)]
        return remote(rows, kr.at[head], kr_ss.at[step], kr_rs.at[step], quad_at(other(step)))

    for step in range(1, QUAD):
        kr_copy(step).start()
    kr[head] = cb[:ROWS]

    for step in range(1, QUAD):
        for copy in (kv_copy, qg_copy, t_copy, dq_copy, ry_copy):
            copy(step).wait_send()

    def drain_late(index, carry):
        @pl.when(index != mate)
        def _():
            for part in range(2):
                ga_send(part, index).wait_send()

        return carry

    lax.fori_loop(run * 2, MATES, drain_late, 0)

    def drain_early(index, carry):
        @pl.when(index != mate)
        def _():
            pb_send(index).wait_send()

        return carry

    lax.fori_loop(0, run * 2 + 2, drain_early, 0)

    for step in range(1, 8):
        rz_copy(step).wait_send()
    for step in range(1, 8):
        rx_copy(step).wait_recv()
    r_sum[...] = sum((rx[number] for number in range(1, 8)), start=rx[0]) * (1.0 / math.sqrt(4 * 2048))
    for step in range(1, QUAD):
        for copy in (dq_copy, kr_copy):
            copy(step).wait_recv()
        kr_copy(step).wait_send()
    for step in range(1, 8):
        rx_copy(step).wait_send()


def finish(dqr, kr, cos_s, sin_s, r_sum, dq_out, dk_out, dv_out, r_out):
    cos = cos_s[...]
    sin = sin_s[...]

    def turn_back(rows):
        return rows * cos - pltpu.roll(rows, HD // 2, 1) * sin

    for number in range(HQ):
        cols = slice((number % GROUP) * HD, (number % GROUP + 1) * HD)
        rows = dqr[number // GROUP, :, cols].astype(F32)
        dq_out[:, number * HD : (number + 1) * HD] = turn_back(rows).astype(BF16)
    for number in range(KVH):
        cols = slice(number * HD, (number + 1) * HD)
        dk_out[:, cols] = turn_back(kr[number, :, :HD].astype(F32)).astype(BF16)
        dv_out[:, cols] = kr[number, :, HD:]
    r_out[...] = r_sum[...]


def shards(queries, keys, values, out_grad, routed_inputs, router_weight, positions):
    vmem = pl.BlockSpec(memory_space=pltpu.VMEM)
    hbm = pl.BlockSpec(memory_space=pltpu.HBM)
    dma = pltpu.SemaphoreType.DMA
    scratch = [
        pltpu.VMEM((ROWS, HQ * HD), BF16),
        pltpu.VMEM((ROWS, KVH * HD), BF16),
        pltpu.VMEM((ROWS, KVH * HD), BF16),
        pltpu.VMEM((ROWS, HQ * HD), BF16),
        pltpu.VMEM((ROWS, 4096), BF16),
        pltpu.VMEM((1, 4096), F32),
        pltpu.VMEM((1, ROWS), jnp.int32),
        pltpu.VMEM((8, HD), F32),
        dma((8,)),
        pltpu.VMEM((ROWS, HD), F32),
        pltpu.VMEM((KVH, ROWS, 2 * HD), BF16),
        pltpu.VMEM((QUAD, 2, ROWS, GROUP * HD), BF16),
        pltpu.VMEM((MATES, SLOT, 2 * HD), BF16),
        pltpu.VMEM((QUAD, 2, ROWS, GROUP * HD), BF16),
        pltpu.VMEM((QROWS, HD), BF16),
        pltpu.VMEM((QROWS, HD), BF16),
        pltpu.VMEM((SUPER, SPAN, QROWS), F32),
        pltpu.VMEM((SUPER, SPAN, QROWS), F32),
        pltpu.VMEM((HD, QROWS), F32),
        pltpu.VMEM((MATES, SLOT, 2 * HD), BF16),
        pltpu.VMEM((MATES, SLOT, 2 * HD), BF16),
        pltpu.VMEM((QUAD, ROWS, GROUP * HD), BF16),
        pltpu.VMEM((SLOT, 2 * HD), BF16),
        pltpu.VMEM((8, 128), F32),
        pltpu.VMEM((QUAD, 8, 128), F32),
        pltpu.VMEM((32, 128), F32),
        pltpu.VMEM((8, 32, 128), F32),
        pltpu.VMEM((32, 128), F32),
        pltpu.VMEM((4, 32, 128), F32),
        pltpu.VMEM((32, 128), F32),
        pltpu.VMEM((8, 32, 128), F32),
        dma((QUAD,)), dma((QUAD,)), dma((QUAD,)), dma((QUAD,)),
        dma((QUAD, MATES)), dma((QUAD, MATES)), dma((MATES,)), dma((MATES,)),
        dma((QUAD,)), dma((QUAD,)), dma((QUAD,)), dma((QUAD,)),
        dma((QUAD,)), dma((QUAD,)), dma((8,)), dma((8,)),
        dma((4,)), dma((4,)), dma((8,)), dma((8,)),
    ]
    landed = pl.pallas_call(
        kernel,
        out_shape=(
            jax.ShapeDtypeStruct((QUAD, ROWS, GROUP * HD), BF16),
            jax.ShapeDtypeStruct((QUAD, ROWS, 2 * HD), BF16),
            jax.ShapeDtypeStruct((ROWS, HD), F32),
            jax.ShapeDtypeStruct((ROWS, HD), F32),
            jax.ShapeDtypeStruct((32, 128), F32),
        ),
        in_specs=[hbm] * 8,
        out_specs=(vmem,) * 5,
        scratch_shapes=scratch,
        compiler_params=pltpu.CompilerParams(
            collective_id=0, has_side_effects=True, vmem_limit_bytes=63 * 1024 * 1024
        ),
    )(
        queries[0],
        keys[0],
        values[0],
        out_grad[0],
        routed_inputs[0],
        router_weight.reshape(1, -1),
        positions,
        jnp.asarray(rope_rows()),
    )
    query_grad, key_grad, value_grad, router = pl.pallas_call(
        finish,
        out_shape=(
            jax.ShapeDtypeStruct((ROWS, HQ * HD), BF16),
            jax.ShapeDtypeStruct((ROWS, KVH * HD), BF16),
            jax.ShapeDtypeStruct((ROWS, KVH * HD), BF16),
            jax.ShapeDtypeStruct((32, 128), F32),
        ),
        in_specs=[vmem] * 5,
        out_specs=(vmem,) * 4,
    )(*landed)
    return (query_grad[None], key_grad[None], value_grad[None], router.reshape(-1))


def solution(mesh):
    row = P("dp", "ctx", None)
    in_specs = (row, row, row, row, row, P(), P("dp", "ctx"))
    out_specs = (row, row, row, P())
    return jax.shard_map(shards, mesh=mesh, in_specs=in_specs, out_specs=out_specs, check_vma=False)
```

```python
import math

import jax
import jax.numpy as jnp
import numpy as np
from jax import lax
from jax.experimental import pallas as pl
from jax.experimental.pallas import tpu as pltpu
from jax.sharding import PartitionSpec as P

HQ = 16
KVH = 4
HD = 128
ROPE_BASE = 500000.0
SCORE_SCALE = 1.0 / math.sqrt(HD)
MESH = pl.DeviceIdType.MESH

ROWS = 32
QUAD = 4
MATES = 16
SUPER = 8
SLOT = QUAD * ROWS
SPAN = 2 * SLOT
GROUP = HQ // KVH
QROWS = GROUP * SLOT
NEG = -1e30
F32 = jnp.float32
BF16 = jnp.bfloat16


def rope_rows():
    pairs = HD // 2
    frequency = [ROPE_BASE ** (-number / pairs) for number in range(pairs)]
    coarse = [256.0 * factor % (2.0 * math.pi) for factor in frequency]
    table = np.zeros((8, HD), np.float32)
    table[0] = np.asarray(frequency + frequency, np.float32)
    table[1] = np.asarray(coarse + coarse, np.float32)
    return table


def nt(left, right):
    return lax.dot_general(left, right, (((1,), (1,)), ((), ())), preferred_element_type=F32)


def tn(left, right):
    return lax.dot_general(left, right, (((0,), (0,)), ((), ())), preferred_element_type=F32)


def kernel(
    q_hbm, k_hbm, v_hbm, g_hbm, x_hbm, w_hbm, p_hbm, rope_hbm,
    dqr, kr, cos_s, sin_s, r_sum,
    q_ref, k_ref, v_ref, g_ref, x_ref, w_ref, p_ref, rope_ref, in_sem, gate_s, kv4, qg4, kv, qg, q_s, g_s, s_s, d_s, dqt_s, pb, rb, dqs, cb,
    ts, tr, rz_s, rz, ry_s, ry, rx_s, rx,
    kv_ss, kv_rs, qg_ss, qg_rs, ga_ss, ga_rs, pb_ss, pb_rs, dq_ss, dq_rs, kr_ss, kr_rs,
    t_ss, t_rs, rz_ss, rz_rs, ry_ss, ry_rs, rx_ss, rx_rs,
):
    dp = lax.axis_index("dp")
    ctx = lax.axis_index("ctx")
    run = ctx // 8
    z = ctx % 8
    head = z // 2
    par = z % 2
    mate = run * 2 + par
    row = run // 2
    side_x = dp * 2 + run % 2

    def quad_at(member):
        return (dp, run * 8 + 2 * member + par)

    def mate_at(index):
        return (dp, (index // 2) * 8 + 2 * head + index % 2)

    def z_at(step):
        return (dp, run * 8 + lax.rem(z + step, 8))

    def y_at(step):
        return (dp, lax.rem(ctx + 16 * step, 64))

    def x_at(step):
        to = lax.rem(side_x + step, 8)
        return (to // 2, (row * 2 + to % 2) * 8 + z)

    def remote(src, dst, send, recv, to):
        return pltpu.make_async_remote_copy(
            src_ref=src, dst_ref=dst, send_sem=send, recv_sem=recv, device_id=to, device_id_type=MESH
        )

    def settle(ref, sem):
        pltpu.make_async_copy(ref, ref, sem).wait()

    def other(step):
        return lax.rem(head + step, QUAD)

    pairs = (
        (p_hbm, p_ref), (rope_hbm, rope_ref), (k_hbm, k_ref), (v_hbm, v_ref),
        (x_hbm, x_ref), (w_hbm, w_ref), (q_hbm, q_ref), (g_hbm, g_ref),
    )
    fetches = [
        pltpu.make_async_copy(src, dst, in_sem.at[number]) for number, (src, dst) in enumerate(pairs)
    ]
    for fetch in fetches:
        fetch.start()

    barrier = pltpu.get_barrier_semaphore()

    def greet_near(step, carry):
        pl.semaphore_signal(barrier, inc=1, device_id=z_at(step), device_id_type=MESH)
        pl.semaphore_signal(barrier, inc=1, device_id=x_at(step), device_id_type=MESH)
        return carry

    lax.fori_loop(1, 8, greet_near, 0)

    def greet(step, carry):
        pl.semaphore_signal(
            barrier, inc=1, device_id=mate_at(lax.rem(mate + step, MATES)), device_id_type=MESH
        )
        return carry

    lax.fori_loop(1, MATES, greet, 0)

    fetches[0].wait()
    fetches[1].wait()

    eye = lax.broadcasted_iota(jnp.int32, (ROWS, ROWS), 0) == lax.broadcasted_iota(
        jnp.int32, (ROWS, ROWS), 1
    )
    places = jnp.broadcast_to(p_ref[...], (ROWS, ROWS))
    upper = jnp.sum(jnp.where(eye, (places >> 8).astype(F32), 0.0), axis=1, keepdims=True)
    lower = jnp.sum(jnp.where(eye, (places & 255).astype(F32), 0.0), axis=1, keepdims=True)
    angles = upper * rope_ref[1:2, :] + lower * rope_ref[0:1, :]
    lane = lax.broadcasted_iota(jnp.int32, (ROWS, HD), 1)
    cos = jnp.cos(angles)
    sin = jnp.sin(angles)
    sin = jnp.where(lane < HD // 2, -sin, sin)
    cos_s[...] = cos
    sin_s[...] = sin

    def turn(rows):
        return rows * cos + pltpu.roll(rows, HD // 2, 1) * sin

    fetches[2].wait()
    fetches[3].wait()
    for number in range(KVH):
        cols = slice(number * HD, (number + 1) * HD)
        kv4[number, :, :HD] = turn(k_ref[:, cols].astype(F32)).astype(BF16)
        kv4[number, :, HD:] = v_ref[:, cols]

    pl.semaphore_wait(barrier, 2 * 7 + MATES - 1)

    def kv_copy(step):
        to = other(step)
        rows = pl.ds((QUAD - step) * ROWS, ROWS)
        return remote(kv4.at[to], kv.at[mate, rows], kv_ss.at[0], kv_rs.at[0], quad_at(to))

    def ga_send(part, index):
        rows = kv.at[mate, pl.ds(part * ROWS, ROWS if part == 0 else 3 * ROWS)]
        return remote(rows, rows, ga_ss.at[0], ga_rs.at[run], mate_at(index))

    def ga_start(part):
        def start(step, carry):
            index = run * 2 + MATES - 1 - step

            @pl.when(index != mate)
            def _():
                ga_send(part, index).start()

            return carry

        lax.fori_loop(run * 2, MATES, start, 0)

    for step in range(1, QUAD):
        kv_copy(step).start()
    kv[mate, :ROWS] = kv4[head]
    ga_start(0)

    for fetch in fetches[4:]:
        fetch.wait()
    logits = jnp.sum(x_ref[...].astype(F32) * w_ref[...], axis=1, keepdims=True)
    gate = jax.nn.sigmoid(logits)
    gate_s[...] = jnp.broadcast_to(gate, (ROWS, HD))
    for number in range(HQ):
        cols = slice(number * HD, (number + 1) * HD)
        part, into = number // GROUP, slice((number % GROUP) * HD, (number % GROUP + 1) * HD)
        qg4[part, 0, :, into] = turn(q_ref[:, cols].astype(F32)).astype(BF16)
        qg4[part, 1, :, into] = (gate * g_ref[:, cols].astype(F32)).astype(BF16)

    def qg_copy(step):
        to = other(step)
        return remote(qg4.at[to], qg.at[head], qg_ss.at[0], qg_rs.at[0], quad_at(to))

    for step in range(1, QUAD):
        qg_copy(step).start()
    qg[head] = qg4[head]

    settle(kv4.at[pl.ds(0, 3)], kv_rs.at[0])
    ga_start(1)

    settle(qg.at[pl.ds(0, 3)], qg_rs.at[0])
    for number in range(GROUP):
        cols = slice(number * HD, (number + 1) * HD)
        q_s[number * SLOT : (number + 1) * SLOT, :] = qg[:, 0, :, cols].reshape(SLOT, HD)
        g_s[number * SLOT : (number + 1) * SLOT, :] = qg[:, 1, :, cols].reshape(SLOT, HD)

    key_at = lax.broadcasted_iota(jnp.int32, (SPAN, QROWS), 0)
    key_at = (key_at >> 7) * ROWS + (((key_at + head * ROWS) & 96) << 1) + (key_at & 31)
    row_at = lax.broadcasted_iota(jnp.int32, (SPAN, QROWS), 1)
    row_at = par * ROWS + ((row_at & 96) << 1) + (row_at & 31)
    ahead = key_at - row_at

    def score_step(back, top):
        number = run - back

        @pl.when(number != run)
        def _():
            settle(kv.at[pl.ds(0, 2)], ga_rs.at[number])

        @pl.when(number == run)
        def _():
            settle(kv.at[0], ga_rs.at[number])

        both = jnp.concatenate([kv[2 * number], kv[2 * number + 1]], axis=0)
        scores = nt(both[:, :HD], q_s[...]) * (SCORE_SCALE * math.log2(math.e))
        scores = jnp.where(ahead <= (run - number) * SPAN, scores, NEG)
        s_s[number] = scores
        d_s[number] = nt(both[:, HD:], g_s[...]) * SCORE_SCALE
        return jnp.maximum(top, jnp.max(scores, axis=0, keepdims=True))

    top = lax.fori_loop(0, run + 1, score_step, jnp.full((1, QROWS), NEG, F32))

    def mass_step(number, carry):
        mass, pull = carry
        raised = jnp.exp2(s_s[number] - top)
        s_s[number] = raised
        return (
            mass + jnp.sum(raised, axis=0, keepdims=True),
            pull + jnp.sum(raised * d_s[number], axis=0, keepdims=True),
        )

    zero_row = jnp.zeros((1, QROWS), F32)
    mass, pull = lax.fori_loop(0, run + 1, mass_step, (zero_row, zero_row))
    inverse = 1.0 / mass
    delta = pull * inverse

    term = delta[:, :SLOT]
    for number in range(1, GROUP):
        term = term + delta[:, number * SLOT : (number + 1) * SLOT]
    ts[...] = jnp.broadcast_to(term * math.sqrt(HD), (8, SLOT))

    def t_copy(step):
        return remote(ts, tr.at[head], t_ss.at[0], t_rs.at[0], quad_at(other(step)))

    for step in range(1, QUAD):
        t_copy(step).start()
    tr[head] = ts[...]

    def pb_send(index):
        return remote(pb.at[index], rb.at[mate], pb_ss.at[0], pb_rs.at[run], mate_at(index))

    dqt_s[...] = jnp.zeros_like(dqt_s)

    def grad_step(number, carry):
        weights = s_s[number] * inverse
        probs = weights.astype(BF16)
        slope = (weights * (d_s[number] - delta)).astype(BF16)
        keys = jnp.concatenate([kv[2 * number, :, :HD], kv[2 * number + 1, :, :HD]], axis=0)
        dk = jnp.dot(slope, q_s[...], preferred_element_type=F32)
        dv = jnp.dot(probs, g_s[...], preferred_element_type=F32)
        grads = jnp.concatenate([dk, dv], axis=1).astype(BF16)
        for side in range(2):
            index = 2 * number + side
            pb[index] = grads[side * SLOT : (side + 1) * SLOT]

            @pl.when(index != mate)
            def _():
                pb_send(index).start()

        dqt_s[...] += tn(keys, slope)
        return carry

    half = (run + 1) // 2
    lax.fori_loop(0, half, grad_step, 0)

    settle(tr.at[pl.ds(0, 3)], t_rs.at[0])
    term = tr[0] + tr[1] + tr[2] + tr[3]
    spot = lax.broadcasted_iota(jnp.int32, (ROWS, SLOT), 0) + head * ROWS
    pick = lax.broadcasted_iota(jnp.int32, (ROWS, SLOT), 1) == spot
    term = jnp.concatenate([term] * (ROWS // 8), axis=0)
    term = jnp.sum(jnp.where(pick, term, 0.0), axis=1, keepdims=True)
    logit_grad = (1.0 - gate_s[:, 0:1]) * term
    part = jnp.sum(logit_grad * x_ref[...].astype(F32), axis=0, keepdims=True)
    for number in range(32):
        rz_s[number : number + 1, :] = part[:, number * 128 : (number + 1) * 128]

    def rz_copy(step):
        return remote(rz_s, rz.at[z], rz_ss.at[0], rz_rs.at[0], z_at(step))

    def ry_copy(step):
        return remote(ry_s, ry.at[row], ry_ss.at[0], ry_rs.at[0], y_at(step))

    def rx_copy(step):
        return remote(rx_s, rx.at[side_x], rx_ss.at[0], rx_rs.at[0], x_at(step))

    for step in range(1, 8):
        rz_copy(step).start()
    rz[z] = rz_s[...]

    lax.fori_loop(half, run + 1, grad_step, 0)

    turned = dqt_s[...].T.astype(BF16)
    for number in range(GROUP):
        cols = slice(number * HD, (number + 1) * HD)
        dqs[:, :, cols] = turned[number * SLOT : (number + 1) * SLOT].reshape(QUAD, ROWS, HD)

    def dq_copy(step):
        to = other(step)
        return remote(dqs.at[to], dqr.at[head], dq_ss.at[0], dq_rs.at[0], quad_at(to))

    for step in range(1, QUAD):
        dq_copy(step).start()
    dqr[head] = dqs[head]

    rb[mate] = pb[mate]

    def gather_sum(number, total):
        @pl.when(number != run)
        def _():
            settle(rb.at[pl.ds(0, 2)], pb_rs.at[number])

        @pl.when(number == run)
        def _():
            settle(rb.at[0], pb_rs.at[number])

        return total + (rb[2 * number].astype(F32) + rb[2 * number + 1].astype(F32))

    settle(rz.at[pl.ds(0, 7)], rz_rs.at[0])
    ry_s[...] = sum((rz[number] for number in range(1, 8)), start=rz[0])
    for step in range(1, 4):
        ry_copy(step).start()
    ry[row] = ry_s[...]

    middle = (run + SUPER) // 2
    total = lax.fori_loop(run, middle, gather_sum, jnp.zeros((SLOT, 2 * HD), F32))

    settle(ry.at[pl.ds(0, 3)], ry_rs.at[0])
    rx_s[...] = ry[0] + ry[1] + ry[2] + ry[3]
    for step in range(1, 8):
        rx_copy(step).start()
    rx[side_x] = rx_s[...]

    total = lax.fori_loop(middle, SUPER, gather_sum, total)
    cb[...] = total.astype(BF16)

    def kr_copy(step):
        rows = cb.at[pl.ds(step * ROWS, ROWS)]
        return remote(rows, kr.at[head], kr_ss.at[0], kr_rs.at[0], quad_at(other(step)))

    for step in range(1, QUAD):
        kr_copy(step).start()
    kr[head] = cb[:ROWS]

    settle(kv4.at[pl.ds(0, 3)], kv_ss.at[0])
    settle(qg.at[pl.ds(0, 3)], qg_ss.at[0])
    settle(tr.at[pl.ds(0, 3)], t_ss.at[0])
    settle(dqr.at[pl.ds(0, 3)], dq_ss.at[0])
    settle(rz.at[pl.ds(0, 7)], rz_ss.at[0])
    settle(ry.at[pl.ds(0, 3)], ry_ss.at[0])
    settle(kv.at[0], ga_ss.at[0])
    settle(pb.at[0], pb_ss.at[0])

    def drain_late(number, carry):
        settle(kv.at[pl.ds(0, 2)], ga_ss.at[0])
        return carry

    def drain_early(number, carry):
        settle(pb.at[pl.ds(0, 2)], pb_ss.at[0])
        return carry

    lax.fori_loop(run + 1, SUPER, drain_late, 0)
    lax.fori_loop(0, run, drain_early, 0)
    settle(rx.at[pl.ds(0, 7)], rx_rs.at[0])
    r_sum[...] = sum((rx[number] for number in range(1, 8)), start=rx[0]) * (1.0 / math.sqrt(4 * 2048))
    settle(dqr.at[pl.ds(0, 3)], dq_rs.at[0])
    settle(kr.at[pl.ds(0, 3)], kr_rs.at[0])
    settle(kr.at[pl.ds(0, 3)], kr_ss.at[0])
    settle(rx.at[pl.ds(0, 7)], rx_ss.at[0])


def finish(dqr, kr, cos_s, sin_s, r_sum, dq_out, dk_out, dv_out, r_out):
    cos = cos_s[...]
    sin = sin_s[...]

    def turn_back(rows):
        return rows * cos - pltpu.roll(rows, HD // 2, 1) * sin

    for number in range(HQ):
        cols = slice((number % GROUP) * HD, (number % GROUP + 1) * HD)
        rows = dqr[number // GROUP, :, cols].astype(F32)
        dq_out[:, number * HD : (number + 1) * HD] = turn_back(rows).astype(BF16)
    for number in range(KVH):
        cols = slice(number * HD, (number + 1) * HD)
        dk_out[:, cols] = turn_back(kr[number, :, :HD].astype(F32)).astype(BF16)
        dv_out[:, cols] = kr[number, :, HD:]
    r_out[...] = r_sum[...]


def shards(queries, keys, values, out_grad, routed_inputs, router_weight, positions):
    vmem = pl.BlockSpec(memory_space=pltpu.VMEM)
    hbm = pl.BlockSpec(memory_space=pltpu.HBM)
    dma = pltpu.SemaphoreType.DMA
    scratch = [
        pltpu.VMEM((ROWS, HQ * HD), BF16),
        pltpu.VMEM((ROWS, KVH * HD), BF16),
        pltpu.VMEM((ROWS, KVH * HD), BF16),
        pltpu.VMEM((ROWS, HQ * HD), BF16),
        pltpu.VMEM((ROWS, 4096), BF16),
        pltpu.VMEM((1, 4096), F32),
        pltpu.VMEM((1, ROWS), jnp.int32),
        pltpu.VMEM((8, HD), F32),
        dma((8,)),
        pltpu.VMEM((ROWS, HD), F32),
        pltpu.VMEM((KVH, ROWS, 2 * HD), BF16),
        pltpu.VMEM((QUAD, 2, ROWS, GROUP * HD), BF16),
        pltpu.VMEM((MATES, SLOT, 2 * HD), BF16),
        pltpu.VMEM((QUAD, 2, ROWS, GROUP * HD), BF16),
        pltpu.VMEM((QROWS, HD), BF16),
        pltpu.VMEM((QROWS, HD), BF16),
        pltpu.VMEM((SUPER, SPAN, QROWS), F32),
        pltpu.VMEM((SUPER, SPAN, QROWS), F32),
        pltpu.VMEM((HD, QROWS), F32),
        pltpu.VMEM((MATES, SLOT, 2 * HD), BF16),
        pltpu.VMEM((MATES, SLOT, 2 * HD), BF16),
        pltpu.VMEM((QUAD, ROWS, GROUP * HD), BF16),
        pltpu.VMEM((SLOT, 2 * HD), BF16),
        pltpu.VMEM((8, 128), F32),
        pltpu.VMEM((QUAD, 8, 128), F32),
        pltpu.VMEM((32, 128), F32),
        pltpu.VMEM((8, 32, 128), F32),
        pltpu.VMEM((32, 128), F32),
        pltpu.VMEM((4, 32, 128), F32),
        pltpu.VMEM((32, 128), F32),
        pltpu.VMEM((8, 32, 128), F32),
        dma((1,)), dma((1,)), dma((1,)), dma((1,)),
        dma((1,)), dma((SUPER,)), dma((1,)), dma((SUPER,)),
        dma((1,)), dma((1,)), dma((1,)), dma((1,)),
        dma((1,)), dma((1,)), dma((1,)), dma((1,)),
        dma((1,)), dma((1,)), dma((1,)), dma((1,)),
    ]
    landed = pl.pallas_call(
        kernel,
        out_shape=(
            jax.ShapeDtypeStruct((QUAD, ROWS, GROUP * HD), BF16),
            jax.ShapeDtypeStruct((QUAD, ROWS, 2 * HD), BF16),
            jax.ShapeDtypeStruct((ROWS, HD), F32),
            jax.ShapeDtypeStruct((ROWS, HD), F32),
            jax.ShapeDtypeStruct((32, 128), F32),
        ),
        in_specs=[hbm] * 8,
        out_specs=(vmem,) * 5,
        scratch_shapes=scratch,
        compiler_params=pltpu.CompilerParams(
            collective_id=0, has_side_effects=True, vmem_limit_bytes=63 * 1024 * 1024
        ),
    )(
        queries[0],
        keys[0],
        values[0],
        out_grad[0],
        routed_inputs[0],
        router_weight.reshape(1, -1),
        positions,
        jnp.asarray(rope_rows()),
    )
    query_grad, key_grad, value_grad, router = pl.pallas_call(
        finish,
        out_shape=(
            jax.ShapeDtypeStruct((ROWS, HQ * HD), BF16),
            jax.ShapeDtypeStruct((ROWS, KVH * HD), BF16),
            jax.ShapeDtypeStruct((ROWS, KVH * HD), BF16),
            jax.ShapeDtypeStruct((32, 128), F32),
        ),
        in_specs=[vmem] * 5,
        out_specs=(vmem,) * 4,
    )(*landed)
    return (query_grad[None], key_grad[None], value_grad[None], router.reshape(-1))


def solution(mesh):
    row = P("dp", "ctx", None)
    in_specs = (row, row, row, row, row, P(), P("dp", "ctx"))
    out_specs = (row, row, row, P())
    return jax.shard_map(shards, mesh=mesh, in_specs=in_specs, out_specs=out_specs, check_vma=False)
```

```python
import math

import jax
import jax.numpy as jnp
import numpy as np
from jax import lax
from jax.experimental import pallas as pl
from jax.experimental.pallas import tpu as pltpu
from jax.sharding import PartitionSpec as P

HQ = 16
KVH = 4
HD = 128
ROPE_BASE = 500000.0
SCORE_SCALE = 1.0 / math.sqrt(HD)
MESH = pl.DeviceIdType.MESH

ROWS = 32
QUAD = 4
MATES = 16
SUPER = 8
SLOT = QUAD * ROWS
SPAN = 2 * SLOT
GROUP = HQ // KVH
QROWS = GROUP * SLOT
NEG = -1e30
F32 = jnp.float32
BF16 = jnp.bfloat16


def rope_rows():
    pairs = HD // 2
    frequency = [ROPE_BASE ** (-number / pairs) for number in range(pairs)]
    coarse = [256.0 * factor % (2.0 * math.pi) for factor in frequency]
    table = np.zeros((8, HD), np.float32)
    table[0] = np.asarray(frequency + frequency, np.float32)
    table[1] = np.asarray(coarse + coarse, np.float32)
    return table


def nt(left, right):
    return lax.dot_general(left, right, (((1,), (1,)), ((), ())), preferred_element_type=F32)


def tn(left, right):
    return lax.dot_general(left, right, (((0,), (0,)), ((), ())), preferred_element_type=F32)


def kernel(
    q_hbm, k_hbm, v_hbm, g_hbm, x_hbm, w_hbm, p_hbm, rope_hbm,
    dqr, kr, cos_s, sin_s, r_sum,
    q_ref, k_ref, v_ref, g_ref, x_ref, w_ref, p_ref, rope_ref, in_sem, gate_s, kv4, qg4, kv, qg, q_s, g_s, s_s, d_s, dqt_s, pb, rb, dqs, cb,
    ts, tr, rz_s, rz, ry_s, ry, rx_s, rx,
    kv_ss, kv_rs, qg_ss, qg_rs, ga_ss, ga_rs, pb_ss, pb_rs, dq_ss, dq_rs, kr_ss, kr_rs,
    t_ss, t_rs, rz_ss, rz_rs, ry_ss, ry_rs, rx_ss, rx_rs,
):
    dp = lax.axis_index("dp")
    ctx = lax.axis_index("ctx")
    run = ctx // 8
    z = ctx % 8
    head = z // 2
    par = z % 2
    mate = run * 2 + par
    row = run // 2
    side_x = dp * 2 + run % 2

    def quad_at(member):
        return (dp, run * 8 + 2 * member + par)

    def mate_at(index):
        return (dp, (index // 2) * 8 + 2 * head + index % 2)

    def z_at(step):
        return (dp, run * 8 + lax.rem(z + step, 8))

    def y_at(step):
        return (dp, lax.rem(ctx + 16 * step, 64))

    def x_at(step):
        to = lax.rem(side_x + step, 8)
        return (to // 2, (row * 2 + to % 2) * 8 + z)

    def remote(src, dst, send, recv, to):
        return pltpu.make_async_remote_copy(
            src_ref=src, dst_ref=dst, send_sem=send, recv_sem=recv, device_id=to, device_id_type=MESH
        )

    def settle(ref, sem):
        pltpu.make_async_copy(ref, ref, sem).wait()

    def ring_sum(slots, count):
        return sum((slots[number].astype(F32) for number in range(1, count)), start=slots[0].astype(F32))

    def other(step):
        return lax.rem(head + step, QUAD)

    pairs = (
        (p_hbm, p_ref), (rope_hbm, rope_ref), (k_hbm, k_ref), (v_hbm, v_ref),
        (x_hbm, x_ref), (w_hbm, w_ref), (q_hbm, q_ref), (g_hbm, g_ref),
    )
    fetches = [
        pltpu.make_async_copy(src, dst, in_sem.at[number]) for number, (src, dst) in enumerate(pairs)
    ]
    for fetch in fetches:
        fetch.start()

    barrier = pltpu.get_barrier_semaphore()

    for step in range(1, 8):
        pl.semaphore_signal(barrier, inc=1, device_id=z_at(step), device_id_type=MESH)
        pl.semaphore_signal(barrier, inc=1, device_id=x_at(step), device_id_type=MESH)
    for step in range(1, MATES):
        to = mate_at(lax.rem(mate + step, MATES))
        pl.semaphore_signal(barrier, inc=1, device_id=to, device_id_type=MESH)

    fetches[0].wait()
    fetches[1].wait()

    eye = lax.broadcasted_iota(jnp.int32, (ROWS, ROWS), 0) == lax.broadcasted_iota(
        jnp.int32, (ROWS, ROWS), 1
    )
    places = jnp.broadcast_to(p_ref[...], (ROWS, ROWS))
    upper = jnp.sum(jnp.where(eye, (places >> 8).astype(F32), 0.0), axis=1, keepdims=True)
    lower = jnp.sum(jnp.where(eye, (places & 255).astype(F32), 0.0), axis=1, keepdims=True)
    angles = upper * rope_ref[1:2, :] + lower * rope_ref[0:1, :]
    lane = lax.broadcasted_iota(jnp.int32, (ROWS, HD), 1)
    cos = jnp.cos(angles)
    sin = jnp.sin(angles)
    sin = jnp.where(lane < HD // 2, -sin, sin)
    cos_s[...] = cos
    sin_s[...] = sin

    def turn(rows):
        return rows * cos + pltpu.roll(rows, HD // 2, 1) * sin

    fetches[2].wait()
    fetches[3].wait()
    for number in range(KVH):
        cols = slice(number * HD, (number + 1) * HD)
        kv4[number, :, :HD] = turn(k_ref[:, cols].astype(F32)).astype(BF16)
        kv4[number, :, HD:] = v_ref[:, cols]

    pl.semaphore_wait(barrier, 2 * 7 + MATES - 1)

    def kv_copy(step):
        to = other(step)
        rows = pl.ds((QUAD - step) * ROWS, ROWS)
        return remote(kv4.at[to], kv.at[mate, rows], kv_ss.at[0], kv_rs.at[0], quad_at(to))

    def ga_send(part, index):
        rows = kv.at[mate, pl.ds(part * ROWS, ROWS if part == 0 else 3 * ROWS)]
        return remote(rows, rows, ga_ss.at[0], ga_rs.at[run], mate_at(index))

    def ga_start(part):
        for number in reversed(range(1, SUPER)):

            @pl.when(number > run)
            def _():
                ga_send(part, 2 * number).start()
                ga_send(part, 2 * number + 1).start()

        ga_send(part, run * 2 + 1 - par).start()

    for step in range(1, QUAD):
        kv_copy(step).start()
    kv[mate, :ROWS] = kv4[head]
    ga_start(0)

    for fetch in fetches[4:]:
        fetch.wait()
    logits = jnp.sum(x_ref[...].astype(F32) * w_ref[...], axis=1, keepdims=True)
    gate = jax.nn.sigmoid(logits)
    gate_s[...] = jnp.broadcast_to(gate, (ROWS, HD))
    for number in range(HQ):
        cols = slice(number * HD, (number + 1) * HD)
        part, into = number // GROUP, slice((number % GROUP) * HD, (number % GROUP + 1) * HD)
        qg4[part, 0, :, into] = turn(q_ref[:, cols].astype(F32)).astype(BF16)
        qg4[part, 1, :, into] = (gate * g_ref[:, cols].astype(F32)).astype(BF16)

    def qg_copy(step):
        to = other(step)
        return remote(qg4.at[to], qg.at[head], qg_ss.at[0], qg_rs.at[0], quad_at(to))

    for step in range(1, QUAD):
        qg_copy(step).start()
    qg[head] = qg4[head]

    settle(kv4.at[pl.ds(0, 3)], kv_rs.at[0])
    ga_start(1)

    settle(qg.at[pl.ds(0, 3)], qg_rs.at[0])
    for number in range(GROUP):
        cols = slice(number * HD, (number + 1) * HD)
        q_s[number * SLOT : (number + 1) * SLOT, :] = qg[:, 0, :, cols].reshape(SLOT, HD)
        g_s[number * SLOT : (number + 1) * SLOT, :] = qg[:, 1, :, cols].reshape(SLOT, HD)

    key_at = lax.broadcasted_iota(jnp.int32, (SPAN, QROWS), 0)
    key_at = (key_at >> 7) * ROWS + (((key_at + head * ROWS) & 96) << 1) + (key_at & 31)
    row_at = lax.broadcasted_iota(jnp.int32, (SPAN, QROWS), 1)
    row_at = par * ROWS + ((row_at & 96) << 1) + (row_at & 31)
    ahead = key_at - row_at

    def score_step(back, carry):
        top, mass, pull = carry
        number = run - back

        @pl.when(number != run)
        def _():
            settle(kv.at[pl.ds(0, 2)], ga_rs.at[number])

        @pl.when(number == run)
        def _():
            settle(kv.at[0], ga_rs.at[number])

        both = jnp.concatenate([kv[2 * number], kv[2 * number + 1]], axis=0)
        scores = nt(both[:, :HD], q_s[...]) * (SCORE_SCALE * math.log2(math.e))
        scores = jnp.where(ahead <= (run - number) * SPAN, scores, NEG)
        s_s[number] = scores
        slopes = nt(both[:, HD:], g_s[...]) * SCORE_SCALE
        d_s[number] = slopes
        higher = jnp.maximum(top, jnp.max(scores, axis=0, keepdims=True))
        fade = jnp.exp2(top - higher)
        raised = jnp.exp2(scores - higher)
        return (
            higher,
            mass * fade + jnp.sum(raised, axis=0, keepdims=True),
            pull * fade + jnp.sum(raised * slopes, axis=0, keepdims=True),
        )

    zero_row = jnp.zeros((1, QROWS), F32)
    lowest = jnp.full((1, QROWS), NEG, F32)
    top, mass, pull = lax.fori_loop(0, run + 1, score_step, (lowest, zero_row, zero_row))

    level = top + jnp.log2(mass)
    delta = pull / mass

    term = delta[:, :SLOT]
    for number in range(1, GROUP):
        term = term + delta[:, number * SLOT : (number + 1) * SLOT]
    ts[...] = jnp.broadcast_to(term * math.sqrt(HD), (8, SLOT))

    def t_copy(step):
        return remote(ts, tr.at[head], t_ss.at[0], t_rs.at[0], quad_at(other(step)))

    for step in range(1, QUAD):
        t_copy(step).start()
    tr[head] = ts[...]

    def pb_send(index):
        return remote(pb.at[index], rb.at[mate], pb_ss.at[0], pb_rs.at[run], mate_at(index))

    dqt_s[...] = jnp.zeros_like(dqt_s)

    def grad_step(number, carry):
        weights = jnp.exp2(s_s[number] - level)
        probs = weights.astype(BF16)
        slope = (weights * (d_s[number] - delta)).astype(BF16)
        keys = jnp.concatenate([kv[2 * number, :, :HD], kv[2 * number + 1, :, :HD]], axis=0)
        dk = jnp.dot(slope, q_s[...], preferred_element_type=F32)
        dv = jnp.dot(probs, g_s[...], preferred_element_type=F32)
        grads = jnp.concatenate([dk, dv], axis=1).astype(BF16)
        for side in range(2):
            index = 2 * number + side
            pb[index] = grads[side * SLOT : (side + 1) * SLOT]

            @pl.when(index != mate)
            def _():
                pb_send(index).start()

        dqt_s[...] += tn(keys, slope)
        return carry

    half = (run + 1) // 2
    lax.fori_loop(0, half, grad_step, 0)

    settle(tr.at[pl.ds(0, 3)], t_rs.at[0])
    term = tr[0] + tr[1] + tr[2] + tr[3]
    spot = lax.broadcasted_iota(jnp.int32, (ROWS, SLOT), 0) + head * ROWS
    pick = lax.broadcasted_iota(jnp.int32, (ROWS, SLOT), 1) == spot
    term = jnp.concatenate([term] * (ROWS // 8), axis=0)
    term = jnp.sum(jnp.where(pick, term, 0.0), axis=1, keepdims=True)
    logit_grad = (1.0 - gate_s[:, 0:1]) * term
    part = jnp.sum(logit_grad * x_ref[...].astype(F32), axis=0, keepdims=True)
    part = jnp.concatenate([part[:, number * 128 : (number + 1) * 128] for number in range(32)], axis=0)
    rz_s[...] = part.astype(BF16)

    def rz_copy(step):
        return remote(rz_s, rz.at[z], rz_ss.at[0], rz_rs.at[0], z_at(step))

    def ry_copy(step):
        return remote(ry_s, ry.at[row], ry_ss.at[0], ry_rs.at[0], y_at(step))

    def rx_copy(step):
        return remote(rx_s, rx.at[side_x], rx_ss.at[0], rx_rs.at[0], x_at(step))

    for step in range(1, 8):
        rz_copy(step).start()
    rz[z] = rz_s[...]

    lax.fori_loop(half, run + 1, grad_step, 0)

    turned = dqt_s[...].T.astype(BF16)
    for number in range(GROUP):
        cols = slice(number * HD, (number + 1) * HD)
        dqs[:, :, cols] = turned[number * SLOT : (number + 1) * SLOT].reshape(QUAD, ROWS, HD)

    def dq_copy(step):
        to = other(step)
        return remote(dqs.at[to], dqr.at[head], dq_ss.at[0], dq_rs.at[0], quad_at(to))

    for step in range(1, QUAD):
        dq_copy(step).start()
    dqr[head] = dqs[head]

    rb[mate] = pb[mate]

    def gather_sum(number, total):
        @pl.when(number != run)
        def _():
            settle(rb.at[pl.ds(0, 2)], pb_rs.at[number])

        @pl.when(number == run)
        def _():
            settle(rb.at[0], pb_rs.at[number])

        return total + (rb[2 * number].astype(F32) + rb[2 * number + 1].astype(F32))

    settle(rz.at[pl.ds(0, 7)], rz_rs.at[0])
    ry_s[...] = ring_sum(rz, 8).astype(BF16)
    for step in range(1, 4):
        ry_copy(step).start()
    ry[row] = ry_s[...]

    middle = (run + SUPER) // 2
    total = lax.fori_loop(run, middle, gather_sum, jnp.zeros((SLOT, 2 * HD), F32))

    settle(ry.at[pl.ds(0, 3)], ry_rs.at[0])
    rx_s[...] = ring_sum(ry, 4).astype(BF16)
    for step in range(1, 8):
        rx_copy(step).start()
    rx[side_x] = rx_s[...]

    total = lax.fori_loop(middle, SUPER, gather_sum, total)
    cb[...] = total.astype(BF16)

    def kr_copy(step):
        rows = cb.at[pl.ds(step * ROWS, ROWS)]
        return remote(rows, kr.at[head], kr_ss.at[0], kr_rs.at[0], quad_at(other(step)))

    for step in range(1, QUAD):
        kr_copy(step).start()
    kr[head] = cb[:ROWS]

    settle(kv4.at[pl.ds(0, 3)], kv_ss.at[0])
    settle(qg.at[pl.ds(0, 3)], qg_ss.at[0])
    settle(tr.at[pl.ds(0, 3)], t_ss.at[0])
    settle(dqr.at[pl.ds(0, 3)], dq_ss.at[0])
    settle(rz.at[pl.ds(0, 7)], rz_ss.at[0])
    settle(ry.at[pl.ds(0, 3)], ry_ss.at[0])
    settle(kv.at[0], ga_ss.at[0])
    settle(pb.at[0], pb_ss.at[0])

    def drain_late(number, carry):
        settle(kv.at[pl.ds(0, 2)], ga_ss.at[0])
        return carry

    def drain_early(number, carry):
        settle(pb.at[pl.ds(0, 2)], pb_ss.at[0])
        return carry

    lax.fori_loop(run + 1, SUPER, drain_late, 0)
    lax.fori_loop(0, run, drain_early, 0)
    settle(rx.at[pl.ds(0, 7)], rx_rs.at[0])
    r_sum[...] = ring_sum(rx, 8) * (1.0 / math.sqrt(4 * 2048))
    settle(dqr.at[pl.ds(0, 3)], dq_rs.at[0])
    settle(kr.at[pl.ds(0, 3)], kr_rs.at[0])
    settle(kr.at[pl.ds(0, 3)], kr_ss.at[0])
    settle(rx.at[pl.ds(0, 7)], rx_ss.at[0])


def finish(dqr, kr, cos_s, sin_s, r_sum, dq_out, dk_out, dv_out, r_out):
    cos = cos_s[...]
    sin = sin_s[...]

    def turn_back(rows):
        return rows * cos - pltpu.roll(rows, HD // 2, 1) * sin

    for number in range(HQ):
        cols = slice((number % GROUP) * HD, (number % GROUP + 1) * HD)
        rows = dqr[number // GROUP, :, cols].astype(F32)
        dq_out[:, number * HD : (number + 1) * HD] = turn_back(rows).astype(BF16)
    for number in range(KVH):
        cols = slice(number * HD, (number + 1) * HD)
        dk_out[:, cols] = turn_back(kr[number, :, :HD].astype(F32)).astype(BF16)
        dv_out[:, cols] = kr[number, :, HD:]
    r_out[...] = r_sum[...]


def shards(queries, keys, values, out_grad, routed_inputs, router_weight, positions):
    vmem = pl.BlockSpec(memory_space=pltpu.VMEM)
    hbm = pl.BlockSpec(memory_space=pltpu.HBM)
    dma = pltpu.SemaphoreType.DMA
    scratch = [
        pltpu.VMEM((ROWS, HQ * HD), BF16),
        pltpu.VMEM((ROWS, KVH * HD), BF16),
        pltpu.VMEM((ROWS, KVH * HD), BF16),
        pltpu.VMEM((ROWS, HQ * HD), BF16),
        pltpu.VMEM((ROWS, 4096), BF16),
        pltpu.VMEM((1, 4096), F32),
        pltpu.VMEM((1, ROWS), jnp.int32),
        pltpu.VMEM((8, HD), F32),
        dma((8,)),
        pltpu.VMEM((ROWS, HD), F32),
        pltpu.VMEM((KVH, ROWS, 2 * HD), BF16),
        pltpu.VMEM((QUAD, 2, ROWS, GROUP * HD), BF16),
        pltpu.VMEM((MATES, SLOT, 2 * HD), BF16),
        pltpu.VMEM((QUAD, 2, ROWS, GROUP * HD), BF16),
        pltpu.VMEM((QROWS, HD), BF16),
        pltpu.VMEM((QROWS, HD), BF16),
        pltpu.VMEM((SUPER, SPAN, QROWS), F32),
        pltpu.VMEM((SUPER, SPAN, QROWS), F32),
        pltpu.VMEM((HD, QROWS), F32),
        pltpu.VMEM((MATES, SLOT, 2 * HD), BF16),
        pltpu.VMEM((MATES, SLOT, 2 * HD), BF16),
        pltpu.VMEM((QUAD, ROWS, GROUP * HD), BF16),
        pltpu.VMEM((SLOT, 2 * HD), BF16),
        pltpu.VMEM((8, 128), F32),
        pltpu.VMEM((QUAD, 8, 128), F32),
        pltpu.VMEM((32, 128), BF16),
        pltpu.VMEM((8, 32, 128), BF16),
        pltpu.VMEM((32, 128), BF16),
        pltpu.VMEM((4, 32, 128), BF16),
        pltpu.VMEM((32, 128), BF16),
        pltpu.VMEM((8, 32, 128), BF16),
        dma((1,)), dma((1,)), dma((1,)), dma((1,)),
        dma((1,)), dma((SUPER,)), dma((1,)), dma((SUPER,)),
        dma((1,)), dma((1,)), dma((1,)), dma((1,)),
        dma((1,)), dma((1,)), dma((1,)), dma((1,)),
        dma((1,)), dma((1,)), dma((1,)), dma((1,)),
    ]
    landed = pl.pallas_call(
        kernel,
        out_shape=(
            jax.ShapeDtypeStruct((QUAD, ROWS, GROUP * HD), BF16),
            jax.ShapeDtypeStruct((QUAD, ROWS, 2 * HD), BF16),
            jax.ShapeDtypeStruct((ROWS, HD), F32),
            jax.ShapeDtypeStruct((ROWS, HD), F32),
            jax.ShapeDtypeStruct((32, 128), F32),
        ),
        in_specs=[hbm] * 8,
        out_specs=(vmem,) * 5,
        scratch_shapes=scratch,
        compiler_params=pltpu.CompilerParams(
            collective_id=0, has_side_effects=True, vmem_limit_bytes=63 * 1024 * 1024
        ),
    )(
        queries[0],
        keys[0],
        values[0],
        out_grad[0],
        routed_inputs[0],
        router_weight.reshape(1, -1),
        positions,
        jnp.asarray(rope_rows()),
    )
    query_grad, key_grad, value_grad, router = pl.pallas_call(
        finish,
        out_shape=(
            jax.ShapeDtypeStruct((ROWS, HQ * HD), BF16),
            jax.ShapeDtypeStruct((ROWS, KVH * HD), BF16),
            jax.ShapeDtypeStruct((ROWS, KVH * HD), BF16),
            jax.ShapeDtypeStruct((32, 128), F32),
        ),
        in_specs=[vmem] * 5,
        out_specs=(vmem,) * 4,
    )(*landed)
    return (query_grad[None], key_grad[None], value_grad[None], router.reshape(-1))


def solution(mesh):
    row = P("dp", "ctx", None)
    in_specs = (row, row, row, row, row, P(), P("dp", "ctx"))
    out_specs = (row, row, row, P())
    return jax.shard_map(shards, mesh=mesh, in_specs=in_specs, out_specs=out_specs, check_vma=False)
```

```python
import math

import jax
import jax.numpy as jnp
import numpy as np
from jax import lax
from jax.experimental import pallas as pl
from jax.experimental.pallas import tpu as pltpu
from jax.sharding import PartitionSpec as P

HQ = 16
KVH = 4
HD = 128
ROPE_BASE = 500000.0
SCORE_SCALE = 1.0 / math.sqrt(HD)
MESH = pl.DeviceIdType.MESH

ROWS = 32
QUAD = 4
MATES = 16
SUPER = 8
SLOT = QUAD * ROWS
SPAN = 2 * SLOT
GROUP = HQ // KVH
QROWS = GROUP * SLOT
NEG = -1e30
F32 = jnp.float32
BF16 = jnp.bfloat16


def rope_rows():
    pairs = HD // 2
    frequency = [ROPE_BASE ** (-number / pairs) for number in range(pairs)]
    coarse = [256.0 * factor % (2.0 * math.pi) for factor in frequency]
    table = np.zeros((8, HD), np.float32)
    table[0] = np.asarray(frequency + frequency, np.float32)
    table[1] = np.asarray(coarse + coarse, np.float32)
    return table


def nt(left, right):
    return lax.dot_general(left, right, (((1,), (1,)), ((), ())), preferred_element_type=F32)


def tn(left, right):
    return lax.dot_general(left, right, (((0,), (0,)), ((), ())), preferred_element_type=F32)


def kernel(
    q_hbm, k_hbm, v_hbm, g_hbm, x_hbm, w_hbm, p_hbm, rope_hbm,
    dqr, kr, cos_s, sin_s, r_sum,
    q_ref, k_ref, v_ref, g_ref, x_ref, w_ref, p_ref, rope_ref, in_sem, gate_s, kv4, qg4, kv, qg, q_s, g_s, s_s, d_s, dqt_s, pb, rb, dqs, cb,
    ts, tr, rz_s, rz, ry_s, ry, rx_s, rx,
    kv_ss, kv_rs, qg_ss, qg_rs, ga_ss, ga_rs, pb_ss, pb_rs, dq_ss, dq_rs, kr_ss, kr_rs,
    t_ss, t_rs, rz_ss, rz_rs, ry_ss, ry_rs, rx_ss, rx_rs,
):
    dp = lax.axis_index("dp")
    ctx = lax.axis_index("ctx")
    run = ctx // 8
    z = ctx % 8
    head = z // 2
    par = z % 2
    mate = run * 2 + par
    core = dp % 2
    spot_xy = run * 2 + dp // 2

    def quad_at(member):
        return (dp, run * 8 + 2 * member + par)

    def mate_at(index):
        return (dp, (index // 2) * 8 + 2 * head + index % 2)

    def z_at(step):
        return (dp, run * 8 + lax.rem(z + step, 8))

    def xy_at(step):
        to = lax.rem(spot_xy + step, 16)
        return (to % 2 * 2 + core, to // 2 * 8 + z)

    twin = (dp + 1 - 2 * core, ctx)

    def remote(src, dst, send, recv, to):
        return pltpu.make_async_remote_copy(
            src_ref=src, dst_ref=dst, send_sem=send, recv_sem=recv, device_id=to, device_id_type=MESH
        )

    def settle(ref, sem):
        pltpu.make_async_copy(ref, ref, sem).wait()

    def ring_sum(slots, count):
        return sum((slots[number].astype(F32) for number in range(1, count)), start=slots[0].astype(F32))

    def other(step):
        return lax.rem(head + step, QUAD)

    pairs = (
        (p_hbm, p_ref), (rope_hbm, rope_ref), (k_hbm, k_ref), (v_hbm, v_ref),
        (x_hbm, x_ref), (w_hbm, w_ref), (q_hbm, q_ref), (g_hbm, g_ref),
    )
    fetches = [
        pltpu.make_async_copy(src, dst, in_sem.at[number]) for number, (src, dst) in enumerate(pairs)
    ]
    for fetch in fetches:
        fetch.start()

    barrier = pltpu.get_barrier_semaphore()

    pl.semaphore_signal(barrier, inc=1, device_id=twin, device_id_type=MESH)
    for step in range(1, 8):
        pl.semaphore_signal(barrier, inc=1, device_id=z_at(step), device_id_type=MESH)
    for step in range(1, 16):
        pl.semaphore_signal(barrier, inc=1, device_id=xy_at(step), device_id_type=MESH)
    for step in range(1, SUPER):
        to = mate_at(lax.rem(run + step, SUPER) * 2 + 1 - par)
        pl.semaphore_signal(barrier, inc=1, device_id=to, device_id_type=MESH)

    fetches[0].wait()
    fetches[1].wait()

    eye = lax.broadcasted_iota(jnp.int32, (ROWS, ROWS), 0) == lax.broadcasted_iota(
        jnp.int32, (ROWS, ROWS), 1
    )
    places = jnp.broadcast_to(p_ref[...], (ROWS, ROWS))
    upper = jnp.sum(jnp.where(eye, (places >> 8).astype(F32), 0.0), axis=1, keepdims=True)
    lower = jnp.sum(jnp.where(eye, (places & 255).astype(F32), 0.0), axis=1, keepdims=True)
    angles = upper * rope_ref[1:2, :] + lower * rope_ref[0:1, :]
    lane = lax.broadcasted_iota(jnp.int32, (ROWS, HD), 1)
    cos = jnp.cos(angles)
    sin = jnp.sin(angles)
    sin = jnp.where(lane < HD // 2, -sin, sin)
    cos_s[...] = cos
    sin_s[...] = sin

    def turn(rows):
        return rows * cos + pltpu.roll(rows, HD // 2, 1) * sin

    fetches[2].wait()
    fetches[3].wait()
    for number in range(KVH):
        cols = slice(number * HD, (number + 1) * HD)
        kv4[number, :, :HD] = turn(k_ref[:, cols].astype(F32)).astype(BF16)
        kv4[number, :, HD:] = v_ref[:, cols]

    pl.semaphore_wait(barrier, 1 + 7 + 15 + SUPER - 1)

    def kv_copy(step):
        to = other(step)
        rows = pl.ds((QUAD - step) * ROWS, ROWS)
        return remote(kv4.at[to], kv.at[mate, rows], kv_ss.at[0], kv_rs.at[0], quad_at(to))

    def ga_send(part, index):
        rows = kv.at[mate, pl.ds(part * ROWS, ROWS if part == 0 else 3 * ROWS)]
        return remote(rows, rows, ga_ss.at[0], ga_rs.at[run], mate_at(index))

    def ga_start(part):
        for number in reversed(range(1, SUPER)):

            @pl.when(number > run)
            def _():
                ga_send(part, 2 * number).start()
                ga_send(part, 2 * number + 1).start()

        ga_send(part, run * 2 + 1 - par).start()

    for step in range(1, QUAD):
        kv_copy(step).start()
    kv[mate, :ROWS] = kv4[head]
    ga_start(0)

    for fetch in fetches[4:]:
        fetch.wait()
    logits = jnp.sum(x_ref[...].astype(F32) * w_ref[...], axis=1, keepdims=True)
    gate = jax.nn.sigmoid(logits)
    gate_s[...] = jnp.broadcast_to(gate, (ROWS, HD))
    for number in range(HQ):
        cols = slice(number * HD, (number + 1) * HD)
        part, into = number // GROUP, slice((number % GROUP) * HD, (number % GROUP + 1) * HD)
        qg4[part, 0, :, into] = turn(q_ref[:, cols].astype(F32)).astype(BF16)
        qg4[part, 1, :, into] = (gate * g_ref[:, cols].astype(F32)).astype(BF16)

    def qg_copy(step):
        to = other(step)
        return remote(qg4.at[to], qg.at[head], qg_ss.at[0], qg_rs.at[0], quad_at(to))

    for step in range(1, QUAD):
        qg_copy(step).start()
    qg[head] = qg4[head]

    settle(kv4.at[pl.ds(0, 3)], kv_rs.at[0])
    ga_start(1)

    settle(qg.at[pl.ds(0, 3)], qg_rs.at[0])
    for number in range(GROUP):
        cols = slice(number * HD, (number + 1) * HD)
        q_s[number * SLOT : (number + 1) * SLOT, :] = qg[:, 0, :, cols].reshape(SLOT, HD)
        g_s[number * SLOT : (number + 1) * SLOT, :] = qg[:, 1, :, cols].reshape(SLOT, HD)

    key_at = lax.broadcasted_iota(jnp.int32, (SPAN, QROWS), 0)
    key_at = (key_at >> 7) * ROWS + (((key_at + head * ROWS) & 96) << 1) + (key_at & 31)
    row_at = lax.broadcasted_iota(jnp.int32, (SPAN, QROWS), 1)
    row_at = par * ROWS + ((row_at & 96) << 1) + (row_at & 31)
    ahead = key_at - row_at

    def score_step(back, carry):
        top, mass, pull = carry
        number = run - back

        @pl.when(number != run)
        def _():
            settle(kv.at[pl.ds(0, 2)], ga_rs.at[number])

        @pl.when(number == run)
        def _():
            settle(kv.at[0], ga_rs.at[number])

        both = jnp.concatenate([kv[2 * number], kv[2 * number + 1]], axis=0)
        scores = nt(both[:, :HD], q_s[...]) * (SCORE_SCALE * math.log2(math.e))
        scores = jnp.where(ahead <= (run - number) * SPAN, scores, NEG)
        s_s[number] = scores
        slopes = nt(both[:, HD:], g_s[...]) * SCORE_SCALE
        d_s[number] = slopes
        higher = jnp.maximum(top, jnp.max(scores, axis=0, keepdims=True))
        fade = jnp.exp2(top - higher)
        raised = jnp.exp2(scores - higher)
        return (
            higher,
            mass * fade + jnp.sum(raised, axis=0, keepdims=True),
            pull * fade + jnp.sum(raised * slopes, axis=0, keepdims=True),
        )

    zero_row = jnp.zeros((1, QROWS), F32)
    lowest = jnp.full((1, QROWS), NEG, F32)
    top, mass, pull = lax.fori_loop(0, run + 1, score_step, (lowest, zero_row, zero_row))

    level = top + jnp.log2(mass)
    delta = pull / mass

    term = delta[:, :SLOT]
    for number in range(1, GROUP):
        term = term + delta[:, number * SLOT : (number + 1) * SLOT]
    ts[...] = jnp.broadcast_to(term * math.sqrt(HD), (8, SLOT))

    def t_copy(step):
        return remote(ts, tr.at[head], t_ss.at[0], t_rs.at[0], quad_at(other(step)))

    for step in range(1, QUAD):
        t_copy(step).start()
    tr[head] = ts[...]

    def pb_send(index):
        return remote(pb.at[index], rb.at[mate], pb_ss.at[0], pb_rs.at[run], mate_at(index))

    dqt_s[...] = jnp.zeros_like(dqt_s)

    def grad_step(number, carry):
        weights = jnp.exp2(s_s[number] - level)
        probs = weights.astype(BF16)
        slope = (weights * (d_s[number] - delta)).astype(BF16)
        keys = jnp.concatenate([kv[2 * number, :, :HD], kv[2 * number + 1, :, :HD]], axis=0)
        dk = jnp.dot(slope, q_s[...], preferred_element_type=F32)
        dv = jnp.dot(probs, g_s[...], preferred_element_type=F32)
        grads = jnp.concatenate([dk, dv], axis=1).astype(BF16)
        for side in range(2):
            index = 2 * number + side
            pb[index] = grads[side * SLOT : (side + 1) * SLOT]

            @pl.when(index != mate)
            def _():
                pb_send(index).start()

        dqt_s[...] += tn(keys, slope)
        return carry

    half = (run + 1) // 2
    lax.fori_loop(0, half, grad_step, 0)

    settle(tr.at[pl.ds(0, 3)], t_rs.at[0])
    term = tr[0] + tr[1] + tr[2] + tr[3]
    spot = lax.broadcasted_iota(jnp.int32, (ROWS, SLOT), 0) + head * ROWS
    pick = lax.broadcasted_iota(jnp.int32, (ROWS, SLOT), 1) == spot
    term = jnp.concatenate([term] * (ROWS // 8), axis=0)
    term = jnp.sum(jnp.where(pick, term, 0.0), axis=1, keepdims=True)
    logit_grad = (1.0 - gate_s[:, 0:1]) * term
    part = jnp.sum(logit_grad * x_ref[...].astype(F32), axis=0, keepdims=True)
    part = jnp.concatenate([part[:, number * 128 : (number + 1) * 128] for number in range(32)], axis=0)
    rz_s[...] = part.astype(BF16)

    def rz_copy(step):
        return remote(rz_s, rz.at[z], rz_ss.at[0], rz_rs.at[0], z_at(step))

    def ry_copy(step):
        return remote(ry_s, ry.at[spot_xy], ry_ss.at[0], ry_rs.at[0], xy_at(step))

    swap = remote(rx_s, rx.at[core], rx_ss.at[0], rx_rs.at[0], twin)

    for step in range(1, 8):
        rz_copy(step).start()
    rz[z] = rz_s[...]

    lax.fori_loop(half, run + 1, grad_step, 0)

    turned = dqt_s[...].T.astype(BF16)
    for number in range(GROUP):
        cols = slice(number * HD, (number + 1) * HD)
        dqs[:, :, cols] = turned[number * SLOT : (number + 1) * SLOT].reshape(QUAD, ROWS, HD)

    def dq_copy(step):
        to = other(step)
        return remote(dqs.at[to], dqr.at[head], dq_ss.at[0], dq_rs.at[0], quad_at(to))

    for step in range(1, QUAD):
        dq_copy(step).start()
    dqr[head] = dqs[head]

    rb[mate] = pb[mate]

    def gather_sum(number, total):
        @pl.when(number != run)
        def _():
            settle(rb.at[pl.ds(0, 2)], pb_rs.at[number])

        @pl.when(number == run)
        def _():
            settle(rb.at[0], pb_rs.at[number])

        return total + (rb[2 * number].astype(F32) + rb[2 * number + 1].astype(F32))

    settle(rz.at[pl.ds(0, 7)], rz_rs.at[0])
    ry_s[...] = ring_sum(rz, 8).astype(BF16)
    for step in range(1, 16):
        ry_copy(step).start()
    ry[spot_xy] = ry_s[...]

    total = lax.fori_loop(run, SUPER, gather_sum, jnp.zeros((SLOT, 2 * HD), F32))
    cb[...] = total.astype(BF16)

    def kr_copy(step):
        rows = cb.at[pl.ds(step * ROWS, ROWS)]
        return remote(rows, kr.at[head], kr_ss.at[0], kr_rs.at[0], quad_at(other(step)))

    for step in range(1, QUAD):
        kr_copy(step).start()
    kr[head] = cb[:ROWS]

    settle(ry.at[pl.ds(0, 15)], ry_rs.at[0])
    rx_s[...] = ring_sum(ry, 16).astype(BF16)
    swap.start()
    rx[core] = rx_s[...]

    settle(kv4.at[pl.ds(0, 3)], kv_ss.at[0])
    settle(qg.at[pl.ds(0, 3)], qg_ss.at[0])
    settle(tr.at[pl.ds(0, 3)], t_ss.at[0])
    settle(dqr.at[pl.ds(0, 3)], dq_ss.at[0])
    settle(rz.at[pl.ds(0, 7)], rz_ss.at[0])
    settle(ry.at[pl.ds(0, 15)], ry_ss.at[0])
    settle(kv.at[0], ga_ss.at[0])
    settle(pb.at[0], pb_ss.at[0])

    def drain_late(number, carry):
        settle(kv.at[pl.ds(0, 2)], ga_ss.at[0])
        return carry

    def drain_early(number, carry):
        settle(pb.at[pl.ds(0, 2)], pb_ss.at[0])
        return carry

    lax.fori_loop(run + 1, SUPER, drain_late, 0)
    lax.fori_loop(0, run, drain_early, 0)
    swap.wait()
    r_sum[...] = ring_sum(rx, 2) * (1.0 / math.sqrt(4 * 2048))
    settle(dqr.at[pl.ds(0, 3)], dq_rs.at[0])
    settle(kr.at[pl.ds(0, 3)], kr_rs.at[0])
    settle(kr.at[pl.ds(0, 3)], kr_ss.at[0])


def finish(dqr, kr, cos_s, sin_s, r_sum, dq_out, dk_out, dv_out, r_out):
    cos = cos_s[...]
    sin = sin_s[...]

    def turn_back(rows):
        return rows * cos - pltpu.roll(rows, HD // 2, 1) * sin

    for number in range(HQ):
        cols = slice((number % GROUP) * HD, (number % GROUP + 1) * HD)
        rows = dqr[number // GROUP, :, cols].astype(F32)
        dq_out[:, number * HD : (number + 1) * HD] = turn_back(rows).astype(BF16)
    for number in range(KVH):
        cols = slice(number * HD, (number + 1) * HD)
        dk_out[:, cols] = turn_back(kr[number, :, :HD].astype(F32)).astype(BF16)
        dv_out[:, cols] = kr[number, :, HD:]
    r_out[...] = r_sum[...]


def shards(queries, keys, values, out_grad, routed_inputs, router_weight, positions):
    vmem = pl.BlockSpec(memory_space=pltpu.VMEM)
    hbm = pl.BlockSpec(memory_space=pltpu.HBM)
    dma = pltpu.SemaphoreType.DMA
    scratch = [
        pltpu.VMEM((ROWS, HQ * HD), BF16),
        pltpu.VMEM((ROWS, KVH * HD), BF16),
        pltpu.VMEM((ROWS, KVH * HD), BF16),
        pltpu.VMEM((ROWS, HQ * HD), BF16),
        pltpu.VMEM((ROWS, 4096), BF16),
        pltpu.VMEM((1, 4096), F32),
        pltpu.VMEM((1, ROWS), jnp.int32),
        pltpu.VMEM((8, HD), F32),
        dma((8,)),
        pltpu.VMEM((ROWS, HD), F32),
        pltpu.VMEM((KVH, ROWS, 2 * HD), BF16),
        pltpu.VMEM((QUAD, 2, ROWS, GROUP * HD), BF16),
        pltpu.VMEM((MATES, SLOT, 2 * HD), BF16),
        pltpu.VMEM((QUAD, 2, ROWS, GROUP * HD), BF16),
        pltpu.VMEM((QROWS, HD), BF16),
        pltpu.VMEM((QROWS, HD), BF16),
        pltpu.VMEM((SUPER, SPAN, QROWS), F32),
        pltpu.VMEM((SUPER, SPAN, QROWS), F32),
        pltpu.VMEM((HD, QROWS), F32),
        pltpu.VMEM((MATES, SLOT, 2 * HD), BF16),
        pltpu.VMEM((MATES, SLOT, 2 * HD), BF16),
        pltpu.VMEM((QUAD, ROWS, GROUP * HD), BF16),
        pltpu.VMEM((SLOT, 2 * HD), BF16),
        pltpu.VMEM((8, 128), F32),
        pltpu.VMEM((QUAD, 8, 128), F32),
        pltpu.VMEM((32, 128), BF16),
        pltpu.VMEM((8, 32, 128), BF16),
        pltpu.VMEM((32, 128), BF16),
        pltpu.VMEM((16, 32, 128), BF16),
        pltpu.VMEM((32, 128), BF16),
        pltpu.VMEM((2, 32, 128), BF16),
        dma((1,)), dma((1,)), dma((1,)), dma((1,)),
        dma((1,)), dma((SUPER,)), dma((1,)), dma((SUPER,)),
        dma((1,)), dma((1,)), dma((1,)), dma((1,)),
        dma((1,)), dma((1,)), dma((1,)), dma((1,)),
        dma((1,)), dma((1,)), dma((1,)), dma((1,)),
    ]
    landed = pl.pallas_call(
        kernel,
        out_shape=(
            jax.ShapeDtypeStruct((QUAD, ROWS, GROUP * HD), BF16),
            jax.ShapeDtypeStruct((QUAD, ROWS, 2 * HD), BF16),
            jax.ShapeDtypeStruct((ROWS, HD), F32),
            jax.ShapeDtypeStruct((ROWS, HD), F32),
            jax.ShapeDtypeStruct((32, 128), F32),
        ),
        in_specs=[hbm] * 8,
        out_specs=(vmem,) * 5,
        scratch_shapes=scratch,
        compiler_params=pltpu.CompilerParams(
            collective_id=0, has_side_effects=True, vmem_limit_bytes=63 * 1024 * 1024
        ),
    )(
        queries[0],
        keys[0],
        values[0],
        out_grad[0],
        routed_inputs[0],
        router_weight.reshape(1, -1),
        positions,
        jnp.asarray(rope_rows()),
    )
    query_grad, key_grad, value_grad, router = pl.pallas_call(
        finish,
        out_shape=(
            jax.ShapeDtypeStruct((ROWS, HQ * HD), BF16),
            jax.ShapeDtypeStruct((ROWS, KVH * HD), BF16),
            jax.ShapeDtypeStruct((ROWS, KVH * HD), BF16),
            jax.ShapeDtypeStruct((32, 128), F32),
        ),
        in_specs=[vmem] * 5,
        out_specs=(vmem,) * 4,
    )(*landed)
    return (query_grad[None], key_grad[None], value_grad[None], router.reshape(-1))


def solution(mesh):
    row = P("dp", "ctx", None)
    in_specs = (row, row, row, row, row, P(), P("dp", "ctx"))
    out_specs = (row, row, row, P())
    return jax.shard_map(shards, mesh=mesh, in_specs=in_specs, out_specs=out_specs, check_vma=False)
```

```python
import math

import jax
import jax.numpy as jnp
import numpy as np
from jax import lax
from jax.experimental import pallas as pl
from jax.experimental.pallas import tpu as pltpu
from jax.sharding import PartitionSpec as P

HQ = 16
KVH = 4
HD = 128
ROPE_BASE = 500000.0
SCORE_SCALE = 1.0 / math.sqrt(HD)
MESH = pl.DeviceIdType.MESH

ROWS = 32
QUAD = 4
MATES = 16
SUPER = 8
SLOT = QUAD * ROWS
SPAN = 2 * SLOT
GROUP = HQ // KVH
QROWS = GROUP * SLOT
NEG = -1e30
F32 = jnp.float32
BF16 = jnp.bfloat16


def rope_rows():
    pairs = HD // 2
    frequency = [ROPE_BASE ** (-number / pairs) for number in range(pairs)]
    coarse = [256.0 * factor % (2.0 * math.pi) for factor in frequency]
    table = np.zeros((8, HD), np.float32)
    table[0] = np.asarray(frequency + frequency, np.float32)
    table[1] = np.asarray(coarse + coarse, np.float32)
    return table


def nt(left, right):
    return lax.dot_general(left, right, (((1,), (1,)), ((), ())), preferred_element_type=F32)


def tn(left, right):
    return lax.dot_general(left, right, (((0,), (0,)), ((), ())), preferred_element_type=F32)


def kernel(
    q_hbm, k_hbm, v_hbm, g_hbm, x_hbm, w_hbm, p_hbm, rope_hbm,
    dq_hbm, dk_hbm, dv_hbm, r_hbm,
    q_ref, k_ref, v_ref, g_ref, x_ref, w_ref, p_ref, rope_ref, in_sem, out_sem, dq_out, dk_out, dv_out, r_out, dqr, kr, cos_s, sin_s, gate_s, kv4, qg4, kv, qg, q_s, g_s, s_s, d_s, dqt_s, pb, rb, dqs, cb,
    ts, tr, rz_s, rz, ry_s, ry, rx_s, rx,
    kv_ss, kv_rs, qg_ss, qg_rs, ga_ss, ga_rs, pb_ss, pb_rs, dq_ss, dq_rs, kr_ss, kr_rs,
    t_ss, t_rs, rz_ss, rz_rs, ry_ss, ry_rs, rx_ss, rx_rs,
):
    dp = lax.axis_index("dp")
    ctx = lax.axis_index("ctx")
    run = ctx // 8
    z = ctx % 8
    head = z // 2
    par = z % 2
    mate = run * 2 + par
    core = dp % 2
    spot_xy = run * 2 + dp // 2

    def quad_at(member):
        return (dp, run * 8 + 2 * member + par)

    def mate_at(index):
        return (dp, (index // 2) * 8 + 2 * head + index % 2)

    def z_at(step):
        return (dp, run * 8 + lax.rem(z + step, 8))

    def xy_at(step):
        to = lax.rem(spot_xy + step, 16)
        return (to % 2 * 2 + core, to // 2 * 8 + z)

    twin = (dp + 1 - 2 * core, ctx)

    def remote(src, dst, send, recv, to):
        return pltpu.make_async_remote_copy(
            src_ref=src, dst_ref=dst, send_sem=send, recv_sem=recv, device_id=to, device_id_type=MESH
        )

    def settle(ref, sem):
        pltpu.make_async_copy(ref, ref, sem).wait()

    def ring_sum(slots, count):
        return sum((slots[number].astype(F32) for number in range(1, count)), start=slots[0].astype(F32))

    def other(step):
        return lax.rem(head + step, QUAD)

    pairs = (
        (p_hbm, p_ref), (rope_hbm, rope_ref), (k_hbm, k_ref), (v_hbm, v_ref),
        (x_hbm, x_ref), (w_hbm, w_ref), (q_hbm, q_ref), (g_hbm, g_ref),
    )
    fetches = [
        pltpu.make_async_copy(src, dst, in_sem.at[number]) for number, (src, dst) in enumerate(pairs)
    ]
    for fetch in fetches:
        fetch.start()

    barrier = pltpu.get_barrier_semaphore()

    pl.semaphore_signal(barrier, inc=1, device_id=twin, device_id_type=MESH)
    for step in range(1, 8):
        pl.semaphore_signal(barrier, inc=1, device_id=z_at(step), device_id_type=MESH)
    for step in range(1, 16):
        pl.semaphore_signal(barrier, inc=1, device_id=xy_at(step), device_id_type=MESH)
    for step in range(1, SUPER):
        to = mate_at(lax.rem(run + step, SUPER) * 2 + 1 - par)
        pl.semaphore_signal(barrier, inc=1, device_id=to, device_id_type=MESH)

    fetches[0].wait()
    fetches[1].wait()

    eye = lax.broadcasted_iota(jnp.int32, (ROWS, ROWS), 0) == lax.broadcasted_iota(
        jnp.int32, (ROWS, ROWS), 1
    )
    places = jnp.broadcast_to(p_ref[...], (ROWS, ROWS))
    upper = jnp.sum(jnp.where(eye, (places >> 8).astype(F32), 0.0), axis=1, keepdims=True)
    lower = jnp.sum(jnp.where(eye, (places & 255).astype(F32), 0.0), axis=1, keepdims=True)
    angles = upper * rope_ref[1:2, :] + lower * rope_ref[0:1, :]
    lane = lax.broadcasted_iota(jnp.int32, (ROWS, HD), 1)
    cos = jnp.cos(angles)
    sin = jnp.sin(angles)
    sin = jnp.where(lane < HD // 2, -sin, sin)
    cos_s[...] = cos
    sin_s[...] = sin

    def turn(rows):
        return rows * cos + pltpu.roll(rows, HD // 2, 1) * sin

    fetches[2].wait()
    fetches[3].wait()
    for number in range(KVH):
        cols = slice(number * HD, (number + 1) * HD)
        kv4[number, :, :HD] = turn(k_ref[:, cols].astype(F32)).astype(BF16)
        kv4[number, :, HD:] = v_ref[:, cols]

    pl.semaphore_wait(barrier, 1 + 7 + 15 + SUPER - 1)

    def kv_copy(step):
        to = other(step)
        rows = pl.ds((QUAD - step) * ROWS, ROWS)
        return remote(kv4.at[to], kv.at[mate, rows], kv_ss.at[0], kv_rs.at[0], quad_at(to))

    def ga_send(part, index):
        rows = kv.at[mate, pl.ds(part * ROWS, ROWS if part == 0 else 3 * ROWS)]
        return remote(rows, rows, ga_ss.at[0], ga_rs.at[run], mate_at(index))

    def ga_whole(index):
        rows = kv.at[mate]
        return remote(rows, rows, ga_ss.at[0], ga_rs.at[run], mate_at(index))

    def ga_start(part):
        for number in reversed(range(1, SUPER)):
            early = number >= 4

            @pl.when(number > run)
            def _():
                for index in (2 * number, 2 * number + 1):
                    if early:
                        ga_send(part, index).start()
                    elif part == 1:
                        ga_whole(index).start()

        if part == 1:
            ga_whole(run * 2 + 1 - par).start()

    for step in range(1, QUAD):
        kv_copy(step).start()
    kv[mate, :ROWS] = kv4[head]
    ga_start(0)

    for fetch in fetches[4:]:
        fetch.wait()
    logits = jnp.sum(x_ref[...].astype(F32) * w_ref[...], axis=1, keepdims=True)
    gate = jax.nn.sigmoid(logits)
    gate_s[...] = jnp.broadcast_to(gate, (ROWS, HD))
    for number in range(HQ):
        cols = slice(number * HD, (number + 1) * HD)
        part, into = number // GROUP, slice((number % GROUP) * HD, (number % GROUP + 1) * HD)
        qg4[part, 0, :, into] = turn(q_ref[:, cols].astype(F32)).astype(BF16)
        qg4[part, 1, :, into] = (gate * g_ref[:, cols].astype(F32)).astype(BF16)

    def qg_copy(step):
        to = other(step)
        return remote(qg4.at[to], qg.at[head], qg_ss.at[0], qg_rs.at[0], quad_at(to))

    for step in range(1, QUAD):
        qg_copy(step).start()
    qg[head] = qg4[head]

    settle(kv4.at[pl.ds(0, 3)], kv_rs.at[0])
    ga_start(1)

    settle(qg.at[pl.ds(0, 3)], qg_rs.at[0])
    for number in range(GROUP):
        cols = slice(number * HD, (number + 1) * HD)
        q_s[number * SLOT : (number + 1) * SLOT, :] = qg[:, 0, :, cols].reshape(SLOT, HD)
        g_s[number * SLOT : (number + 1) * SLOT, :] = qg[:, 1, :, cols].reshape(SLOT, HD)

    key_at = lax.broadcasted_iota(jnp.int32, (SPAN, QROWS), 0)
    key_at = (key_at >> 7) * ROWS + (((key_at + head * ROWS) & 96) << 1) + (key_at & 31)
    row_at = lax.broadcasted_iota(jnp.int32, (SPAN, QROWS), 1)
    row_at = par * ROWS + ((row_at & 96) << 1) + (row_at & 31)
    ahead = key_at - row_at

    def score_step(back, carry):
        top, mass, pull = carry
        number = run - back

        @pl.when(number != run)
        def _():
            settle(kv.at[pl.ds(0, 2)], ga_rs.at[number])

        @pl.when(number == run)
        def _():
            settle(kv.at[0], ga_rs.at[number])

        both = jnp.concatenate([kv[2 * number], kv[2 * number + 1]], axis=0)
        scores = nt(both[:, :HD], q_s[...]) * (SCORE_SCALE * math.log2(math.e))
        scores = jnp.where(ahead <= (run - number) * SPAN, scores, NEG)
        s_s[number] = scores
        slopes = nt(both[:, HD:], g_s[...]) * SCORE_SCALE
        d_s[number] = slopes
        higher = jnp.maximum(top, jnp.max(scores, axis=0, keepdims=True))
        fade = jnp.exp2(top - higher)
        raised = jnp.exp2(scores - higher)
        return (
            higher,
            mass * fade + jnp.sum(raised, axis=0, keepdims=True),
            pull * fade + jnp.sum(raised * slopes, axis=0, keepdims=True),
        )

    zero_row = jnp.zeros((1, QROWS), F32)
    lowest = jnp.full((1, QROWS), NEG, F32)
    top, mass, pull = lax.fori_loop(0, run + 1, score_step, (lowest, zero_row, zero_row))

    level = top + jnp.log2(mass)
    delta = pull / mass

    term = delta[:, :SLOT]
    for number in range(1, GROUP):
        term = term + delta[:, number * SLOT : (number + 1) * SLOT]
    ts[...] = jnp.broadcast_to(term * math.sqrt(HD), (8, SLOT))

    def t_copy(step):
        return remote(ts, tr.at[head], t_ss.at[0], t_rs.at[0], quad_at(other(step)))

    for step in range(1, QUAD):
        t_copy(step).start()
    tr[head] = ts[...]

    def pb_send(index):
        return remote(pb.at[index], rb.at[mate], pb_ss.at[0], pb_rs.at[run], mate_at(index))

    dqt_s[...] = jnp.zeros_like(dqt_s)

    def grad_step(number, carry):
        weights = jnp.exp2(s_s[number] - level)
        probs = weights.astype(BF16)
        slope = (weights * (d_s[number] - delta)).astype(BF16)
        keys = jnp.concatenate([kv[2 * number, :, :HD], kv[2 * number + 1, :, :HD]], axis=0)
        dk = jnp.dot(slope, q_s[...], preferred_element_type=F32)
        dv = jnp.dot(probs, g_s[...], preferred_element_type=F32)
        grads = jnp.concatenate([dk, dv], axis=1).astype(BF16)
        for side in range(2):
            index = 2 * number + side
            pb[index] = grads[side * SLOT : (side + 1) * SLOT]

            @pl.when(index != mate)
            def _():
                pb_send(index).start()

        dqt_s[...] += tn(keys, slope)
        return carry

    half = (run + 1) // 2
    lax.fori_loop(0, half, grad_step, 0)

    settle(tr.at[pl.ds(0, 3)], t_rs.at[0])
    term = tr[0] + tr[1] + tr[2] + tr[3]
    spot = lax.broadcasted_iota(jnp.int32, (ROWS, SLOT), 0) + head * ROWS
    pick = lax.broadcasted_iota(jnp.int32, (ROWS, SLOT), 1) == spot
    term = jnp.concatenate([term] * (ROWS // 8), axis=0)
    term = jnp.sum(jnp.where(pick, term, 0.0), axis=1, keepdims=True)
    logit_grad = (1.0 - gate_s[:, 0:1]) * term
    part = jnp.sum(logit_grad * x_ref[...].astype(F32), axis=0, keepdims=True)
    part = jnp.concatenate([part[:, number * 128 : (number + 1) * 128] for number in range(32)], axis=0)
    rz_s[...] = part.astype(BF16)

    def rz_copy(step):
        return remote(rz_s, rz.at[z], rz_ss.at[0], rz_rs.at[0], z_at(step))

    def ry_copy(step):
        return remote(ry_s, ry.at[spot_xy], ry_ss.at[0], ry_rs.at[0], xy_at(step))

    swap = remote(rx_s, rx.at[core], rx_ss.at[0], rx_rs.at[0], twin)

    for step in range(1, 8):
        rz_copy(step).start()
    rz[z] = rz_s[...]

    lax.fori_loop(half, run + 1, grad_step, 0)

    turned = dqt_s[...].T.astype(BF16)
    for number in range(GROUP):
        cols = slice(number * HD, (number + 1) * HD)
        dqs[:, :, cols] = turned[number * SLOT : (number + 1) * SLOT].reshape(QUAD, ROWS, HD)

    def dq_copy(step):
        to = other(step)
        return remote(dqs.at[to], dqr.at[head], dq_ss.at[0], dq_rs.at[0], quad_at(to))

    for step in range(1, QUAD):
        dq_copy(step).start()
    dqr[head] = dqs[head]

    rb[mate] = pb[mate]

    def gather_sum(number, total):
        @pl.when(number != run)
        def _():
            settle(rb.at[pl.ds(0, 2)], pb_rs.at[number])

        @pl.when(number == run)
        def _():
            settle(rb.at[0], pb_rs.at[number])

        return total + (rb[2 * number].astype(F32) + rb[2 * number + 1].astype(F32))

    settle(rz.at[pl.ds(0, 7)], rz_rs.at[0])
    ry_s[...] = ring_sum(rz, 8).astype(BF16)
    for step in range(1, 16):
        ry_copy(step).start()
    ry[spot_xy] = ry_s[...]

    total = lax.fori_loop(run, SUPER, gather_sum, jnp.zeros((SLOT, 2 * HD), F32))
    cb[...] = total.astype(BF16)

    def kr_copy(step):
        rows = cb.at[pl.ds(step * ROWS, ROWS)]
        return remote(rows, kr.at[head], kr_ss.at[0], kr_rs.at[0], quad_at(other(step)))

    for step in range(1, QUAD):
        kr_copy(step).start()
    kr[head] = cb[:ROWS]

    back_cos = cos_s[...]
    back_sin = sin_s[...]

    def turn_back(rows):
        return rows * back_cos - pltpu.roll(rows, HD // 2, 1) * back_sin

    results = ((dq_out, dq_hbm), (dk_out, dk_hbm), (dv_out, dv_hbm), (r_out, r_hbm))
    stores = [
        pltpu.make_async_copy(src, dst, out_sem.at[number]) for number, (src, dst) in enumerate(results)
    ]
    settle(dqr.at[pl.ds(0, 3)], dq_rs.at[0])
    for number in range(HQ):
        cols = slice((number % GROUP) * HD, (number % GROUP + 1) * HD)
        rows = dqr[number // GROUP, :, cols].astype(F32)
        dq_out[:, number * HD : (number + 1) * HD] = turn_back(rows).astype(BF16)
    stores[0].start()
    settle(ry.at[pl.ds(0, 15)], ry_rs.at[0])
    rx_s[...] = ring_sum(ry, 16).astype(BF16)
    swap.start()
    rx[core] = rx_s[...]

    settle(kv4.at[pl.ds(0, 3)], kv_ss.at[0])
    settle(qg.at[pl.ds(0, 3)], qg_ss.at[0])
    settle(tr.at[pl.ds(0, 3)], t_ss.at[0])
    settle(dqr.at[pl.ds(0, 3)], dq_ss.at[0])
    settle(rz.at[pl.ds(0, 7)], rz_ss.at[0])
    settle(ry.at[pl.ds(0, 15)], ry_ss.at[0])
    settle(kv.at[0], ga_ss.at[0])
    settle(pb.at[0], pb_ss.at[0])

    def drain_late(number, carry):
        settle(kv.at[pl.ds(0, 2)], ga_ss.at[0])
        return carry

    def drain_early(number, carry):
        settle(pb.at[pl.ds(0, 2)], pb_ss.at[0])
        return carry

    lax.fori_loop(run + 1, SUPER, drain_late, 0)
    lax.fori_loop(0, run, drain_early, 0)

    swap.wait()
    r_out[...] = ring_sum(rx, 2) * (1.0 / math.sqrt(4 * 2048))
    stores[3].start()
    settle(kr.at[pl.ds(0, 3)], kr_rs.at[0])
    for number in range(KVH):
        cols = slice(number * HD, (number + 1) * HD)
        dk_out[:, cols] = turn_back(kr[number, :, :HD].astype(F32)).astype(BF16)
        dv_out[:, cols] = kr[number, :, HD:]
    stores[1].start()
    stores[2].start()
    settle(kr.at[pl.ds(0, 3)], kr_ss.at[0])
    for store in stores:
        store.wait()


def finish(dq_in, dk_in, dv_in, r_in, dq_out, dk_out, dv_out, r_out):
    dq_out[...] = dq_in[...]
    dk_out[...] = dk_in[...]
    dv_out[...] = dv_in[...]
    r_out[...] = r_in[...]


def shards(queries, keys, values, out_grad, routed_inputs, router_weight, positions):
    vmem = pl.BlockSpec(memory_space=pltpu.VMEM)
    hbm = pl.BlockSpec(memory_space=pltpu.HBM)
    dma = pltpu.SemaphoreType.DMA
    scratch = [
        pltpu.VMEM((ROWS, HQ * HD), BF16),
        pltpu.VMEM((ROWS, KVH * HD), BF16),
        pltpu.VMEM((ROWS, KVH * HD), BF16),
        pltpu.VMEM((ROWS, HQ * HD), BF16),
        pltpu.VMEM((ROWS, 4096), BF16),
        pltpu.VMEM((1, 4096), F32),
        pltpu.VMEM((1, ROWS), jnp.int32),
        pltpu.VMEM((8, HD), F32),
        dma((8,)),
        dma((4,)),
        pltpu.VMEM((ROWS, HQ * HD), BF16),
        pltpu.VMEM((ROWS, KVH * HD), BF16),
        pltpu.VMEM((ROWS, KVH * HD), BF16),
        pltpu.VMEM((32, 128), F32),
        pltpu.VMEM((QUAD, ROWS, GROUP * HD), BF16),
        pltpu.VMEM((QUAD, ROWS, 2 * HD), BF16),
        pltpu.VMEM((ROWS, HD), F32),
        pltpu.VMEM((ROWS, HD), F32),
        pltpu.VMEM((ROWS, HD), F32),
        pltpu.VMEM((KVH, ROWS, 2 * HD), BF16),
        pltpu.VMEM((QUAD, 2, ROWS, GROUP * HD), BF16),
        pltpu.VMEM((MATES, SLOT, 2 * HD), BF16),
        pltpu.VMEM((QUAD, 2, ROWS, GROUP * HD), BF16),
        pltpu.VMEM((QROWS, HD), BF16),
        pltpu.VMEM((QROWS, HD), BF16),
        pltpu.VMEM((SUPER, SPAN, QROWS), F32),
        pltpu.VMEM((SUPER, SPAN, QROWS), F32),
        pltpu.VMEM((HD, QROWS), F32),
        pltpu.VMEM((MATES, SLOT, 2 * HD), BF16),
        pltpu.VMEM((MATES, SLOT, 2 * HD), BF16),
        pltpu.VMEM((QUAD, ROWS, GROUP * HD), BF16),
        pltpu.VMEM((SLOT, 2 * HD), BF16),
        pltpu.VMEM((8, 128), F32),
        pltpu.VMEM((QUAD, 8, 128), F32),
        pltpu.VMEM((32, 128), BF16),
        pltpu.VMEM((8, 32, 128), BF16),
        pltpu.VMEM((32, 128), BF16),
        pltpu.VMEM((16, 32, 128), BF16),
        pltpu.VMEM((32, 128), BF16),
        pltpu.VMEM((2, 32, 128), BF16),
        dma((1,)), dma((1,)), dma((1,)), dma((1,)),
        dma((1,)), dma((SUPER,)), dma((1,)), dma((SUPER,)),
        dma((1,)), dma((1,)), dma((1,)), dma((1,)),
        dma((1,)), dma((1,)), dma((1,)), dma((1,)),
        dma((1,)), dma((1,)), dma((1,)), dma((1,)),
    ]
    results = (
        jax.ShapeDtypeStruct((ROWS, HQ * HD), BF16),
        jax.ShapeDtypeStruct((ROWS, KVH * HD), BF16),
        jax.ShapeDtypeStruct((ROWS, KVH * HD), BF16),
        jax.ShapeDtypeStruct((32, 128), F32),
    )
    held = pl.pallas_call(
        kernel,
        out_shape=results,
        in_specs=[hbm] * 8,
        out_specs=(hbm,) * 4,
        scratch_shapes=scratch,
        compiler_params=pltpu.CompilerParams(
            collective_id=0, has_side_effects=True, vmem_limit_bytes=63 * 1024 * 1024
        ),
    )(
        queries[0],
        keys[0],
        values[0],
        out_grad[0],
        routed_inputs[0],
        router_weight.reshape(1, -1),
        positions,
        jnp.asarray(rope_rows()),
    )
    query_grad, key_grad, value_grad, router = pl.pallas_call(
        finish,
        out_shape=results,
        in_specs=[vmem] * 4,
        out_specs=(vmem,) * 4,
    )(*held)
    return (query_grad[None], key_grad[None], value_grad[None], router.reshape(-1))


def solution(mesh):
    row = P("dp", "ctx", None)
    in_specs = (row, row, row, row, row, P(), P("dp", "ctx"))
    out_specs = (row, row, row, P())
    return jax.shard_map(shards, mesh=mesh, in_specs=in_specs, out_specs=out_specs, check_vma=False)
```
